32 devices in a mesh: ctx: 4 (over z), tp: 8 (over y, x, core).
Axes of the slice: x: 2, y: 2, z: 4, core: 2. Of those that a mesh axis runs over, the one named last changes fastest.
Arguments:
- inputs: bfloat16 [1024, 8192], P(('ctx', 'tp')), may hold values from -6 to 6
- query_weight: bfloat16 [8192, 8192], P(None, 'tp'), may hold values from -0.0625 to 0.0625
- key_weight: bfloat16 [8192, 8192], P(None, 'tp'), may hold values from -0.0625 to 0.0625
- value_weight: bfloat16 [8192, 8192], P(None, 'tp'), may hold values from -0.0625 to 0.0625
- filter_taps: float32 [128, 8192], P(None, 'tp'), may hold values from -0.45 to 0.45
- out_grad: bfloat16 [1024, 8192], P('ctx', 'tp'), may hold values from -1.5 to 1.5
Outputs:
- mixed: bfloat16 [1024, 8192], P('ctx', 'tp')
- inputs_grad: bfloat16 [1024, 8192], P(('ctx', 'tp'))
- filter_grad: float32 [128, 8192], P(None, 'tp')
The draws below stay inside these ranges and needn't reach their ends.
All inputs are finite; a program needn't handle non-finite values.
Results may differ from the reference program's by a relative error of at most 0.025.
Values may be sent and summed in bfloat16 or wider, within the bound.
No kernel may reach another device: no remote copies, remote signals or barrier semaphores. Data moves between devices by JAX's collectives and lax.ppermute only.
A program may use at most 128 MiB of HBM per device.

```python
import jax
import jax.numpy as jnp
from jax import lax

D = 8192
TAPS = 128
TOKENS = 1024
N_TP = 8


def block_levels(own_key, dims, split, low, high):
    level = 1.0
    for dim, shards_of in split:
        steps = jax.random.uniform(jax.random.fold_in(jax.random.fold_in(own_key, 6), dim), (shards_of,), jnp.float32, low / len(split), high / len(split))
        level = level * jnp.repeat(jnp.exp(steps), dims[dim] // shards_of).reshape((-1,) + (1,) * (len(dims) - 1 - dim))
    return level


def noise(own_key, dims, scale, most, pieces=(), held_as=jnp.bfloat16):
    values = jax.random.normal(own_key, dims, jnp.float32) * scale
    if len(pieces) > 0:
        values = block_levels(own_key, dims, pieces, -0.22, 0.18) * values
    return jnp.clip(values, min=-most, max=most).astype(held_as)


def setup_inputs(seed: int = 0) -> dict:
    streams_of = jax.random.split(jax.random.key(seed), 7)
    inputs = noise(streams_of[0], (TOKENS, D), 1.0, 6.0, ((0, 32),))
    query_weight = noise(streams_of[1], (D, D), D ** -0.5, 0.0625, ((1, 8),))
    key_weight = noise(streams_of[2], (D, D), D ** -0.5, 0.0625, ((1, 8),))
    value_weight = noise(streams_of[3], (D, D), D ** -0.5, 0.0625, ((1, 8),))
    filter_taps = noise(streams_of[4], (TAPS, D), 0.09, 0.45, ((1, 8),), jnp.float32)
    out_grad = noise(streams_of[5], (TOKENS, D), 0.25, 1.5, ((0, 4), (1, 8)))
    return {"inputs": inputs, "query_weight": query_weight, "key_weight": key_weight, "value_weight": value_weight, "filter_taps": filter_taps, "out_grad": out_grad}


def forward_filter(padded, filter_taps, length):
    taps = filter_taps.shape[0]
    total = jnp.zeros((length, padded.shape[1]), jnp.float32)
    for offset in range(taps):
        start = taps - 1 - offset
        total = total + filter_taps[offset] * padded[start:start + length]
    return total


def backward_filter(padded, filter_taps, length):
    taps = filter_taps.shape[0]
    total = jnp.zeros((length, padded.shape[1]), jnp.float32)
    for offset in range(taps):
        total = total + filter_taps[offset] * padded[offset:offset + length]
    return total


def tap_products(grad_rows, padded, taps, length):
    rows_out = []
    for offset in range(taps):
        start = taps - 1 - offset
        rows_out.append(jnp.sum(grad_rows * padded[start:start + length], axis=0))
    return jnp.stack(rows_out)


def reference(inputs, query_weight, key_weight, value_weight, filter_taps, out_grad):
    length = inputs.shape[0]
    width = inputs.shape[1]
    taps = filter_taps.shape[0]
    margin = taps - 1
    query = jnp.dot(inputs, query_weight, preferred_element_type=jnp.float32).astype(jnp.bfloat16)
    keys = jnp.dot(inputs, key_weight, preferred_element_type=jnp.float32).astype(jnp.bfloat16)
    values = jnp.dot(inputs, value_weight, preferred_element_type=jnp.float32).astype(jnp.bfloat16)
    product = (keys.astype(jnp.float32) * values.astype(jnp.float32)).astype(jnp.bfloat16)
    padded_prod = jnp.concatenate([jnp.zeros((margin, width), jnp.float32), product.astype(jnp.float32)], axis=0)
    conv = forward_filter(padded_prod, filter_taps, length)
    mixed = (query.astype(jnp.float32) * conv).astype(jnp.bfloat16)
    grad_f32 = out_grad.astype(jnp.float32)
    conv_in_grad = (grad_f32 * query.astype(jnp.float32)).astype(jnp.bfloat16)
    query_grad = (grad_f32 * conv).astype(jnp.bfloat16)
    padded_grad = jnp.concatenate([conv_in_grad.astype(jnp.float32), jnp.zeros((margin, width), jnp.float32)], axis=0)
    product_grad = backward_filter(padded_grad, filter_taps, length)
    keys_grad = (product_grad * values.astype(jnp.float32)).astype(jnp.bfloat16)
    values_grad = (product_grad * keys.astype(jnp.float32)).astype(jnp.bfloat16)
    filter_grad = tap_products(conv_in_grad.astype(jnp.float32), padded_prod, taps, length)
    group = width // N_TP

    def columns(array, index):
        return lax.dynamic_slice_in_dim(array, index * group, group, 1)

    def contract(left, right):
        return lax.dot_general(left, right, (((1,), (1,)), ((), ())), preferred_element_type=jnp.float32)

    def add_group(index, total):
        partial_sum = contract(columns(query_grad, index), columns(query_weight, index))
        partial_sum = partial_sum + contract(columns(keys_grad, index), columns(key_weight, index))
        partial_sum = partial_sum + contract(columns(values_grad, index), columns(value_weight, index))
        rounded = lax.optimization_barrier(partial_sum.astype(jnp.bfloat16))
        return total + rounded.astype(jnp.float32)

    summed = lax.fori_loop(0, N_TP, add_group, jnp.zeros((length, width), jnp.float32))
    return mixed, summed.astype(jnp.bfloat16), filter_grad
```

```python
import jax
import jax.numpy as jnp
import numpy as np
from jax import lax
from jax.experimental import pallas as pl
from jax.experimental.pallas import tpu as pltpu
from jax.sharding import PartitionSpec as P

F32 = jnp.float32
BF16 = jnp.bfloat16
VMEM_BYTES = 56 * 2**20
FWD_CHUNKS = 2
BWD_CHUNKS = 2
EXACT = True


def from_behind(block, axis, distance):
    devices = range(lax.axis_size(axis))
    route = [(i - distance, i) for i in devices if i - distance in devices]
    return lax.ppermute(block, axis, route)


def swap(block, way):
    offsets = {0: (1, 1), 1: (2, 4), 2: (4, 2)}[way]
    return lax.ppermute(block, "tp", [(i, i ^ offsets[i % 2]) for i in range(8)])


def row_order(tp, paired):
    if not paired:
        return jnp.arange(tp, dtype=jnp.int32)
    me = lax.axis_index("tp").astype(jnp.int32)
    odd = me % 2
    first = 2 + 2 * odd
    second = 6 - first
    own = [me, me ^ first, me ^ second, me ^ 6]
    other = me ^ 1
    return jnp.stack(own + [other, other ^ second, other ^ first, other ^ 6])


def gather_rows(block, paired):
    if not paired:
        return [lax.all_gather(block, "tp", axis=0, tiled=True)]
    near = jnp.concatenate([block, swap(block, 1)], axis=0)
    far = swap(near, 2)
    return [near, far, swap(near, 0), swap(far, 0)]


def scatter_rows(parts, own_rows, paired):
    if not paired:
        return lax.psum_scatter(parts[0], "tp", scatter_dimension=0, tiled=True)
    keep, give = parts
    total = (keep.astype(F32) + swap(give, 0).astype(F32)).astype(BF16)
    mine, first = total[:own_rows], total[own_rows : 2 * own_rows]
    far = swap(total[2 * own_rows :], 2)
    first = (first.astype(F32) + far[own_rows:].astype(F32)).astype(BF16)
    return (mine.astype(F32) + far[:own_rows].astype(F32) + swap(first, 1).astype(F32)).astype(BF16)


def step_rows(depth):
    step = 1024
    while depth % step:
        step //= 2
    return step


def forward_chunk(pieces, weights, start, depth, acc, last, order, out_grad, taps):
    rows = sum(p.shape[0] for p in pieces)
    group = weights[0].shape[1]
    step = step_rows(depth)
    steps = depth // step
    blocks = order.shape[0]
    own = rows // blocks
    n_x = len(pieces)
    has_acc = acc is not None

    def kernel(*refs):
        order_ref, refs = refs[0], refs[1:]
        x_refs, w_refs, refs = refs[:n_x], refs[n_x : n_x + 3], refs[n_x + 3 :]
        if has_acc:
            acc_in, refs = refs[0], refs[1:]
        if last:
            grad_ref, refs = refs[0], refs[1:]
            q_ref, k_ref, v_ref, prod_ref, cig_ref, tail_ref, head_ref = refs[:7]
            total, x_buf, w_buf, x_sem, w_sem = refs[7:]
        else:
            total, x_buf, w_buf, x_sem, w_sem = refs

        def weight_copy(k, m):
            return pltpu.make_async_copy(
                w_refs[m].at[pl.ds(start + k * step, step), :], w_buf.at[k, m], w_sem.at[k, m]
            )

        at, x_copies = 0, []
        for i, piece in enumerate(x_refs):
            x_copies.append(
                pltpu.make_async_copy(piece, x_buf.at[pl.ds(at, piece.shape[0]), :], x_sem.at[i])
            )
            at += piece.shape[0]
        for copy in x_copies:
            copy.start()
        for k in range(steps):
            for m in range(3):
                weight_copy(k, m).start()
        if has_acc:
            total[...] = acc_in[...]
        else:
            total[...] = jnp.zeros_like(total)
        for copy in x_copies:
            copy.wait()

        def body(k, carry):
            x = x_buf[:, pl.ds(pl.multiple_of(k * step, step), step)]
            for m in range(3):
                weight_copy(k, m).wait()
                total[:, m * group : (m + 1) * group] += jnp.dot(x, w_buf[k, m], preferred_element_type=F32)
            return carry

        lax.fori_loop(0, steps, body, 0)
        if last:
            for b in range(blocks):
                here = pl.ds(pl.multiple_of(order_ref[b] * own, own), own)
                part = [total[b * own : (b + 1) * own, m * group : (m + 1) * group].astype(BF16) for m in range(3)]
                q_ref[here, :], k_ref[here, :], v_ref[here, :] = part
                query, keys, values = [p.astype(F32) for p in part]
                prod_ref[here, :] = (keys * values).astype(BF16)
                cig_ref[here, :] = (grad_ref[here, :].astype(F32) * query).astype(BF16)
            tail_ref[...] = prod_ref[rows - taps :, :]
            head_ref[...] = cig_ref[:taps, :]

    vmem, anywhere = pl.BlockSpec(memory_space=pltpu.VMEM), pl.BlockSpec(memory_space=pl.ANY)
    in_specs = [pl.BlockSpec(memory_space=pltpu.SMEM)] + [anywhere] * (n_x + 3)
    args = [order, *pieces, *weights]
    if has_acc:
        in_specs.append(vmem)
        args.append(acc)
    scratch = [
        pltpu.VMEM((rows, depth), BF16),
        pltpu.VMEM((steps, 3, step, group), BF16),
        pltpu.SemaphoreType.DMA((n_x,)),
        pltpu.SemaphoreType.DMA((steps, 3)),
    ]
    full = jax.ShapeDtypeStruct((rows, group), BF16)
    edge = jax.ShapeDtypeStruct((taps, group), BF16)
    if last:
        in_specs.append(vmem)
        args.append(out_grad)
        out_shape = [full] * 5 + [edge] * 2
        scratch = [pltpu.VMEM((rows, 3 * group), F32)] + scratch
    else:
        out_shape = [jax.ShapeDtypeStruct((rows, 3 * group), F32)]
    return pl.pallas_call(
        kernel,
        in_specs=in_specs,
        out_specs=[vmem] * len(out_shape),
        out_shape=out_shape,
        scratch_shapes=scratch,
        compiler_params=pltpu.CompilerParams(vmem_limit_bytes=VMEM_BYTES),
        cost_estimate=pl.CostEstimate(
            flops=6 * rows * depth * group, bytes_accessed=6 * depth * group, transcendentals=0
        ),
        name="project",
    )(*args)


def halves(matrix):
    high = matrix.astype(jnp.bfloat16)
    low = (matrix - high.astype(np.float64)).astype(jnp.bfloat16)
    return high, low


def transforms(length, taps):
    size = length + taps
    angle = 2 * np.pi / size * np.outer(np.arange(size // 2) + 0.5, np.arange(size))
    there = np.concatenate([np.cos(angle), -np.sin(angle)], axis=0)
    back = there.T * (2.0 / size)
    lags = back[np.arange(taps, 0, -1)]
    rows = np.concatenate([back[taps:], back[:length], lags], axis=0)
    return [*halves(there), *halves(rows)]


def middle(query, keys, values, product, conv_in_grad, before, after, filter_taps, out_grad, order):
    length, group = query.shape
    taps = filter_taps.shape[0]
    half = (length + taps) // 2
    width = min(256, group)
    blocks = order.shape[0]
    own = length // blocks
    mats = [jnp.asarray(m) for m in transforms(length, taps)]

    def kernel(order_ref, th_ref, tl_ref, bh_ref, bl_ref, q_ref, k_ref, v_ref, p_ref, c_ref, before_ref, after_ref,
               taps_ref, grad_ref, mixed_ref, qg_ref, kg_ref, vg_ref, fg_ref, sq, sk, sv):
        def there(x, start):
            stop = start + x.shape[0]
            y = jnp.dot(th_ref[:, start:stop], x, preferred_element_type=F32)
            if EXACT:
                y = y + jnp.dot(tl_ref[:, start:stop], x, preferred_element_type=F32)
            return y

        def back(start, stop, re, im):
            y = jnp.concatenate([re, im], axis=0)
            high = y.astype(BF16)
            out = jnp.dot(bh_ref[start:stop, :], high, preferred_element_type=F32)
            if EXACT:
                low = (y - high.astype(F32)).astype(BF16)
                out = out + jnp.dot(bh_ref[start:stop, :], low, preferred_element_type=F32)
                out = out + jnp.dot(bl_ref[start:stop, :], high, preferred_element_type=F32)
            return out

        f = taps_ref[...]
        f_high = f.astype(BF16)
        h = there(f_high, 0)
        if EXACT:
            f_low = (f - f_high.astype(F32)).astype(BF16)
            h = h + jnp.dot(th_ref[:, :taps], f_low, preferred_element_type=F32)
        hr, hi = h[:half], h[half:]
        p = there(p_ref[...], taps) + there(before_ref[...], 0)
        pr, pi = p[:half], p[half:]
        c = there(c_ref[...], 0)
        cr, ci = c[:half], c[half:]
        g = c + there(after_ref[...], length)
        gr, gi = g[:half], g[half:]
        conv = back(0, length, pr * hr - pi * hi, pr * hi + pi * hr)
        product_grad = back(length, 2 * length, hr * gr + hi * gi, hr * gi - hi * gr)
        fg_ref[...] = back(2 * length, 2 * length + taps, cr * pr + ci * pi, cr * pi - ci * pr).astype(BF16)
        mixed_ref[...] = (q_ref[...].astype(F32) * conv).astype(BF16)
        sq[...] = (grad_ref[...].astype(F32) * conv).astype(BF16)
        sk[...] = (product_grad * v_ref[...].astype(F32)).astype(BF16)
        sv[...] = (product_grad * k_ref[...].astype(F32)).astype(BF16)
        for b in range(blocks):
            here = pl.ds(pl.multiple_of(order_ref[b] * own, own), own)
            to = slice(b * own, (b + 1) * own)
            qg_ref[to, :] = sq[here, :]
            kg_ref[to, :] = sk[here, :]
            vg_ref[to, :] = sv[here, :]

    def whole(a):
        return pl.BlockSpec(a.shape, lambda i: (0, 0))

    def cols(a):
        return pl.BlockSpec((a.shape[0], width), lambda i: (0, i))

    arrays = [query, keys, values, product, conv_in_grad, before, after, filter_taps, out_grad]
    full = jax.ShapeDtypeStruct((length, group), BF16)
    outs = [full] * 4 + [jax.ShapeDtypeStruct((taps, group), BF16)]
    return pl.pallas_call(
        kernel,
        grid=(group // width,),
        in_specs=[pl.BlockSpec(memory_space=pltpu.SMEM)] + [whole(m) for m in mats] + [cols(a) for a in arrays],
        out_specs=[cols(a) for a in outs],
        out_shape=outs,
        scratch_shapes=[pltpu.VMEM((length, width), BF16)] * 3,
        compiler_params=pltpu.CompilerParams(vmem_limit_bytes=VMEM_BYTES),
        cost_estimate=pl.CostEstimate(flops=3 * 10**9, bytes_accessed=8 * 10**6, transcendentals=0),
        name="filter",
    )(order, *mats, *arrays)


def backward_chunk(grads, weights, start, depth, parts):
    rows, group = grads[0].shape
    step = step_rows(depth)
    steps = depth // step
    share = rows // parts

    def kernel(*refs):
        g_refs, w_refs, out_refs = refs[:3], refs[3:6], refs[6 : 6 + parts]
        w_buf, w_sem = refs[6 + parts :]

        def weight_copy(k, m):
            return pltpu.make_async_copy(
                w_refs[m].at[pl.ds(start + k * step, step), :], w_buf.at[k, m], w_sem.at[k, m]
            )

        for k in range(steps):
            for m in range(3):
                weight_copy(k, m).start()

        def body(k, carry):
            total = None
            for m in range(3):
                weight_copy(k, m).wait()
                term = lax.dot_general(
                    g_refs[m][...], w_buf[k, m], (((1,), (1,)), ((), ())), preferred_element_type=F32
                )
                total = term if total is None else total + term
            at = pl.ds(pl.multiple_of(k * step, step), step)
            for i in range(parts):
                out_refs[i][:, at] = total[i * share : (i + 1) * share].astype(BF16)
            return carry

        lax.fori_loop(0, steps, body, 0)

    vmem, anywhere = pl.BlockSpec(memory_space=pltpu.VMEM), pl.BlockSpec(memory_space=pl.ANY)
    return pl.pallas_call(
        kernel,
        in_specs=[vmem] * 3 + [anywhere] * 3,
        out_specs=[vmem] * parts,
        out_shape=[jax.ShapeDtypeStruct((share, depth), BF16)] * parts,
        scratch_shapes=[
            pltpu.VMEM((steps, 3, step, group), BF16),
            pltpu.SemaphoreType.DMA((steps, 3)),
        ],
        compiler_params=pltpu.CompilerParams(vmem_limit_bytes=VMEM_BYTES),
        cost_estimate=pl.CostEstimate(
            flops=6 * rows * depth * group, bytes_accessed=6 * depth * group, transcendentals=0
        ),
        name="project_back",
    )(*grads, *weights)


def on_device(inputs, query_weight, key_weight, value_weight, filter_taps, out_grad):
    weights = (query_weight, key_weight, value_weight)
    tp = lax.axis_size("tp")
    paired = tp == 8
    own_rows, width = inputs.shape
    taps = filter_taps.shape[0]
    order = row_order(tp, paired)
    depth = width // FWD_CHUNKS
    acc = None
    for i in range(FWD_CHUNKS):
        pieces = gather_rows(inputs[:, i * depth : (i + 1) * depth], paired)
        last = i == FWD_CHUNKS - 1
        out = forward_chunk(pieces, weights, i * depth, depth, acc, last, order, out_grad, taps)
        acc = out[0]
    query, keys, values, product, conv_in_grad, tail, head = out
    before = from_behind(tail, "ctx", 1)
    after = from_behind(head, "ctx", -1)
    mixed, query_grad, keys_grad, values_grad, local_taps = middle(
        query, keys, values, product, conv_in_grad, before, after, filter_taps, out_grad, order
    )
    filter_grad = lax.psum(local_taps, "ctx").astype(F32)
    depth = width // BWD_CHUNKS
    summed = []
    for i in range(BWD_CHUNKS):
        parts = backward_chunk(
            (query_grad, keys_grad, values_grad), weights, i * depth, depth, 2 if paired else 1
        )
        summed.append(scatter_rows(parts, own_rows, paired))
    return mixed, jnp.concatenate(summed, axis=1), filter_grad


def solution(mesh):
    in_specs = (
        P(("ctx", "tp"), None),
        P(None, "tp"),
        P(None, "tp"),
        P(None, "tp"),
        P(None, "tp"),
        P("ctx", "tp"),
    )
    out_specs = (P("ctx", "tp"), P(("ctx", "tp"), None), P(None, "tp"))
    return jax.shard_map(
        on_device, mesh=mesh, in_specs=in_specs, out_specs=out_specs, check_vma=False
    )
```

```python
import jax
import jax.numpy as jnp
import numpy as np
from jax import lax
from jax.experimental import pallas as pl
from jax.experimental.pallas import tpu as pltpu
from jax.sharding import PartitionSpec as P

F32 = jnp.float32
BF16 = jnp.bfloat16
FWD_VMEM = 46 * 2**20
BWD_VMEM = 46 * 2**20
MID_VMEM = 28 * 2**20
SLOTS = 3
FWD_CHUNKS = 2
BWD_CHUNKS = 2
EXACT = True


def from_behind(block, axis, distance):
    devices = range(lax.axis_size(axis))
    route = [(i - distance, i) for i in devices if i - distance in devices]
    return lax.ppermute(block, axis, route)


def swap(block, way):
    offsets = {0: (1, 1), 1: (2, 4), 2: (4, 2)}[way]
    return lax.ppermute(block, "tp", [(i, i ^ offsets[i % 2]) for i in range(8)])


def row_order(tp, paired):
    if not paired:
        return list(range(tp))
    me = lax.axis_index("tp")
    first = 2 + 2 * (me % 2)
    second = 6 - first
    own = [me, me ^ first, me ^ second, me ^ 6]
    other = me ^ 1
    return own + [other, other ^ second, other ^ first, other ^ 6]


def block_rows(index, own):
    start = index * own
    return pl.ds(start if isinstance(start, int) else pl.multiple_of(start, own), own)


def sum_over(block, axis):
    size = lax.axis_size(axis)
    if size & (size - 1):
        return lax.psum(block, axis).astype(F32)
    total, distance = block.astype(F32), 1
    while distance < size:
        route = [(i, i ^ distance) for i in range(size)]
        mine = total.astype(BF16)
        total = mine.astype(F32) + lax.ppermute(mine, axis, route).astype(F32)
        distance *= 2
    return total


def gather_rows(block, paired):
    if not paired:
        return [lax.all_gather(block, "tp", axis=0, tiled=True)]
    near = jnp.concatenate([block, swap(block, 1)], axis=0)
    far = swap(near, 2)
    return [near, far, swap(near, 0), swap(far, 0)]


def scatter_rows(parts, own_rows, paired):
    if not paired:
        return lax.psum_scatter(parts[0], "tp", scatter_dimension=0, tiled=True)
    keep, give = parts
    total = (keep.astype(F32) + swap(give, 0).astype(F32)).astype(BF16)
    mine, first = total[:own_rows], total[own_rows : 2 * own_rows]
    far = swap(total[2 * own_rows :], 2)
    first = (first.astype(F32) + far[own_rows:].astype(F32)).astype(BF16)
    return (mine.astype(F32) + far[:own_rows].astype(F32) + swap(first, 1).astype(F32)).astype(BF16)


def step_rows(depth):
    step = 512
    while depth % step:
        step //= 2
    return step


def stream_weights(w_refs, w_buf, w_sem, start, step, steps, compute):
    def copy(k, m):
        slot = lax.rem(k, SLOTS)
        rows = pl.ds(start + k * step, step)
        return pltpu.make_async_copy(w_refs[m].at[rows, :], w_buf.at[slot, m], w_sem.at[slot, m])

    for k in range(min(SLOTS - 1, steps)):
        for m in range(3):
            copy(k, m).start()

    def body(k, carry):
        @pl.when(k + SLOTS - 1 < steps)
        def _():
            for m in range(3):
                copy(k + SLOTS - 1, m).start()

        for m in range(3):
            copy(k, m).wait()
        compute(k, lax.rem(k, SLOTS))
        return carry

    return lambda: lax.fori_loop(0, steps, body, 0)


def weight_scratch(step, group):
    return [pltpu.VMEM((SLOTS, 3, step, group), BF16), pltpu.SemaphoreType.DMA((SLOTS, 3))]


def forward_chunk(pieces, weights, start, depth, acc, last, tp, paired, out_grad, taps):
    rows = sum(p.shape[0] for p in pieces)
    group = weights[0].shape[1]
    step = step_rows(depth)
    own = rows // tp
    n_x = len(pieces)
    has_acc = acc is not None

    def kernel(*refs):
        x_refs, w_refs, refs = refs[:n_x], refs[n_x : n_x + 3], refs[n_x + 3 :]
        if has_acc:
            acc_in, refs = refs[0], refs[1:]
        if last:
            grad_ref, refs = refs[0], refs[1:]
            q_ref, k_ref, v_ref, prod_ref, cig_ref, tail_ref, head_ref = refs[:7]
            total, x_buf, w_buf, w_sem = refs[7:]
        else:
            total, x_buf, w_buf, w_sem = refs

        def compute(k, slot):
            x = x_buf[:, pl.ds(pl.multiple_of(k * step, step), step)]
            for m in range(3):
                total[:, m * group : (m + 1) * group] += jnp.dot(x, w_buf[slot, m], preferred_element_type=F32)

        run = stream_weights(w_refs, w_buf, w_sem, start, step, depth // step, compute)
        at = 0
        for piece in x_refs:
            x_buf[at : at + piece.shape[0], :] = piece[...]
            at += piece.shape[0]
        total[...] = acc_in[...] if has_acc else jnp.zeros_like(total)
        run()
        if last:
            for b, index in enumerate(row_order(tp, paired)):
                here = block_rows(index, own)
                part = [total[b * own : (b + 1) * own, m * group : (m + 1) * group].astype(BF16) for m in range(3)]
                q_ref[here, :], k_ref[here, :], v_ref[here, :] = part
                query, keys, values = [p.astype(F32) for p in part]
                prod_ref[here, :] = (keys * values).astype(BF16)
                cig_ref[here, :] = (grad_ref[here, :].astype(F32) * query).astype(BF16)
            tail_ref[...] = prod_ref[rows - taps :, :]
            head_ref[...] = cig_ref[:taps, :]

    vmem, anywhere = pl.BlockSpec(memory_space=pltpu.VMEM), pl.BlockSpec(memory_space=pl.ANY)
    in_specs = [vmem] * n_x + [anywhere] * 3
    args = [*pieces, *weights]
    if has_acc:
        in_specs.append(vmem)
        args.append(acc)
    scratch = [pltpu.VMEM((rows, depth), BF16), *weight_scratch(step, group)]
    full = jax.ShapeDtypeStruct((rows, group), BF16)
    edge = jax.ShapeDtypeStruct((taps, group), BF16)
    if last:
        in_specs.append(vmem)
        args.append(out_grad)
        out_shape = [full] * 5 + [edge] * 2
        scratch = [pltpu.VMEM((rows, 3 * group), F32)] + scratch
    else:
        out_shape = [jax.ShapeDtypeStruct((rows, 3 * group), F32)]
    return pl.pallas_call(
        kernel,
        in_specs=in_specs,
        out_specs=[vmem] * len(out_shape),
        out_shape=out_shape,
        scratch_shapes=scratch,
        compiler_params=pltpu.CompilerParams(vmem_limit_bytes=FWD_VMEM),
        cost_estimate=pl.CostEstimate(
            flops=6 * rows * depth * group, bytes_accessed=6 * depth * group, transcendentals=0
        ),
        name="project",
    )(*args)


def halves(matrix):
    high = matrix.astype(jnp.bfloat16)
    low = (matrix - high.astype(np.float64)).astype(jnp.bfloat16)
    return high, low


def transforms(length, taps):
    size = length + taps
    angle = 2 * np.pi / size * np.outer(np.arange(size // 2) + 0.5, np.arange(size))
    there = np.concatenate([np.cos(angle), -np.sin(angle)], axis=0)
    back = there.T * (2.0 / size)
    lags = back[np.arange(taps, 0, -1)]
    rows = np.concatenate([back[taps:], back[:length], lags], axis=0)
    return [*halves(there), *halves(rows)]


def middle(query, keys, values, product, conv_in_grad, before, after, filter_taps, out_grad, tp, paired):
    length, group = query.shape
    taps = filter_taps.shape[0]
    half = (length + taps) // 2
    width = min(256, group)
    own = length // tp
    mats = [jnp.asarray(m) for m in transforms(length, taps)]

    def kernel(th_ref, tl_ref, bh_ref, bl_ref, q_ref, k_ref, v_ref, p_ref, c_ref, before_ref, after_ref,
               taps_ref, grad_ref, mixed_ref, qg_ref, kg_ref, vg_ref, fg_ref, sq, sk, sv):
        def there(x, start):
            stop = start + x.shape[0]
            y = jnp.dot(th_ref[:, start:stop], x, preferred_element_type=F32)
            if EXACT:
                y = y + jnp.dot(tl_ref[:, start:stop], x, preferred_element_type=F32)
            return y

        def back(start, stop, re, im):
            y = jnp.concatenate([re, im], axis=0)
            high = y.astype(BF16)
            out = jnp.dot(bh_ref[start:stop, :], high, preferred_element_type=F32)
            if EXACT:
                low = (y - high.astype(F32)).astype(BF16)
                out = out + jnp.dot(bh_ref[start:stop, :], low, preferred_element_type=F32)
                out = out + jnp.dot(bl_ref[start:stop, :], high, preferred_element_type=F32)
            return out

        f = taps_ref[...]
        f_high = f.astype(BF16)
        h = there(f_high, 0)
        if EXACT:
            f_low = (f - f_high.astype(F32)).astype(BF16)
            h = h + jnp.dot(th_ref[:, :taps], f_low, preferred_element_type=F32)
        hr, hi = h[:half], h[half:]
        p = there(p_ref[...], taps) + there(before_ref[...], 0)
        pr, pi = p[:half], p[half:]
        c = there(c_ref[...], 0)
        cr, ci = c[:half], c[half:]
        g = c + there(after_ref[...], length)
        gr, gi = g[:half], g[half:]
        conv = back(0, length, pr * hr - pi * hi, pr * hi + pi * hr)
        product_grad = back(length, 2 * length, hr * gr + hi * gi, hr * gi - hi * gr)
        fg_ref[...] = back(2 * length, 2 * length + taps, cr * pr + ci * pi, cr * pi - ci * pr).astype(BF16)
        mixed_ref[...] = (q_ref[...].astype(F32) * conv).astype(BF16)
        sq[...] = (grad_ref[...].astype(F32) * conv).astype(BF16)
        sk[...] = (product_grad * v_ref[...].astype(F32)).astype(BF16)
        sv[...] = (product_grad * k_ref[...].astype(F32)).astype(BF16)
        for b, index in enumerate(row_order(tp, paired)):
            here = block_rows(index, own)
            to = slice(b * own, (b + 1) * own)
            qg_ref[to, :] = sq[here, :]
            kg_ref[to, :] = sk[here, :]
            vg_ref[to, :] = sv[here, :]

    def whole(a):
        return pl.BlockSpec(a.shape, lambda i: (0, 0))

    def cols(a):
        return pl.BlockSpec((a.shape[0], width), lambda i: (0, i))

    arrays = [query, keys, values, product, conv_in_grad, before, after, filter_taps, out_grad]
    full = jax.ShapeDtypeStruct((length, group), BF16)
    outs = [full] * 4 + [jax.ShapeDtypeStruct((taps, group), BF16)]
    return pl.pallas_call(
        kernel,
        grid=(group // width,),
        in_specs=[whole(m) for m in mats] + [cols(a) for a in arrays],
        out_specs=[cols(a) for a in outs],
        out_shape=outs,
        scratch_shapes=[pltpu.VMEM((length, width), BF16)] * 3,
        compiler_params=pltpu.CompilerParams(vmem_limit_bytes=MID_VMEM),
        cost_estimate=pl.CostEstimate(flops=3 * 10**9, bytes_accessed=8 * 10**6, transcendentals=0),
        name="filter",
    )(*mats, *arrays)


def backward_chunk(grads, weights, start, depth, parts):
    rows, group = grads[0].shape
    step = step_rows(depth)
    share = rows // parts

    def kernel(*refs):
        g_refs, w_refs, out_refs = refs[:3], refs[3:6], refs[6 : 6 + parts]
        w_buf, w_sem = refs[6 + parts :]

        def compute(k, slot):
            total = None
            for m in range(3):
                term = lax.dot_general(
                    g_refs[m][...], w_buf[slot, m], (((1,), (1,)), ((), ())), preferred_element_type=F32
                )
                total = term if total is None else total + term
            at = pl.ds(pl.multiple_of(k * step, step), step)
            for i in range(parts):
                out_refs[i][:, at] = total[i * share : (i + 1) * share].astype(BF16)

        stream_weights(w_refs, w_buf, w_sem, start, step, depth // step, compute)()

    vmem, anywhere = pl.BlockSpec(memory_space=pltpu.VMEM), pl.BlockSpec(memory_space=pl.ANY)
    return pl.pallas_call(
        kernel,
        in_specs=[vmem] * 3 + [anywhere] * 3,
        out_specs=[vmem] * parts,
        out_shape=[jax.ShapeDtypeStruct((share, depth), BF16)] * parts,
        scratch_shapes=weight_scratch(step, group),
        compiler_params=pltpu.CompilerParams(vmem_limit_bytes=BWD_VMEM),
        cost_estimate=pl.CostEstimate(
            flops=6 * rows * depth * group, bytes_accessed=6 * depth * group, transcendentals=0
        ),
        name="project_back",
    )(*grads, *weights)


def on_device(inputs, query_weight, key_weight, value_weight, filter_taps, out_grad):
    weights = (query_weight, key_weight, value_weight)
    tp = lax.axis_size("tp")
    paired = tp == 8
    own_rows, width = inputs.shape
    taps = filter_taps.shape[0]
    depth = width // FWD_CHUNKS
    acc = None
    for i in range(FWD_CHUNKS):
        pieces = gather_rows(inputs[:, i * depth : (i + 1) * depth], paired)
        last = i == FWD_CHUNKS - 1
        out = forward_chunk(pieces, weights, i * depth, depth, acc, last, tp, paired, out_grad, taps)
        acc = out[0]
    query, keys, values, product, conv_in_grad, tail, head = out
    before = from_behind(tail, "ctx", 1)
    after = from_behind(head, "ctx", -1)
    mixed, query_grad, keys_grad, values_grad, local_taps = middle(
        query, keys, values, product, conv_in_grad, before, after, filter_taps, out_grad, tp, paired
    )
    filter_grad = sum_over(local_taps, "ctx")
    depth = width // BWD_CHUNKS
    summed = []
    for i in range(BWD_CHUNKS):
        parts = backward_chunk(
            (query_grad, keys_grad, values_grad), weights, i * depth, depth, 2 if paired else 1
        )
        summed.append(scatter_rows(parts, own_rows, paired))
    return mixed, jnp.concatenate(summed, axis=1), filter_grad


def solution(mesh):
    in_specs = (
        P(("ctx", "tp"), None),
        P(None, "tp"),
        P(None, "tp"),
        P(None, "tp"),
        P(None, "tp"),
        P("ctx", "tp"),
    )
    out_specs = (P("ctx", "tp"), P(("ctx", "tp"), None), P(None, "tp"))
    return jax.shard_map(
        on_device, mesh=mesh, in_specs=in_specs, out_specs=out_specs, check_vma=False
    )
```

```python
import math

import jax
import jax.numpy as jnp
import numpy as np
from jax import lax
from jax.experimental import pallas as pl
from jax.experimental.pallas import tpu as pltpu
from jax.sharding import PartitionSpec as P

F32 = jnp.float32
BF16 = jnp.bfloat16
FWD_VMEM = 42 * 2**20
BWD_VMEM = 42 * 2**20
MID_VMEM = 24 * 2**20
SLOTS = 3
FWD_PARTS = (4, 4)
BWD_PARTS = (4, 2, 2)
EXACT = True


def bounds(width, parts):
    edges = np.cumsum((0,) + parts) * width // sum(parts)
    return [(int(a), int(b)) for a, b in zip(edges[:-1], edges[1:])]


def from_behind(block, axis, distance):
    devices = range(lax.axis_size(axis))
    route = [(i - distance, i) for i in devices if i - distance in devices]
    return lax.ppermute(block, axis, route)


def swap(block, way):
    offsets = {0: (1, 1), 1: (2, 4), 2: (4, 2)}[way]
    return lax.ppermute(block, "tp", [(i, i ^ offsets[i % 2]) for i in range(8)])


def row_order(tp, paired):
    if not paired:
        return list(range(tp))
    me = lax.axis_index("tp")
    first = 2 + 2 * (me % 2)
    second = 6 - first
    own = [me, me ^ first, me ^ second, me ^ 6]
    other = me ^ 1
    return own + [other, other ^ second, other ^ first, other ^ 6]


def block_rows(index, own):
    start = index * own
    return pl.ds(start if isinstance(start, int) else pl.multiple_of(start, own), own)


def gather_rows(block, chunks, paired):
    if not paired:
        return [[lax.all_gather(block[:, a:b], "tp", axis=0, tiled=True)] for a, b in chunks]
    first = swap(block, 1)
    pieces = []
    for a, b in chunks:
        near = jnp.concatenate([block[:, a:b], first[:, a:b]], axis=0)
        far = swap(near, 2)
        pieces.append([near, far, swap(near, 0), swap(far, 0)])
    return pieces


def scatter_rows(pieces, totals, own):
    far, first, count = [], [], len(pieces)
    for i in range(count + 1):
        if i < count:
            if i >= len(totals):
                keep, give = pieces[i]
                theirs = swap(give, 0)
                totals.append(add_up(keep, once(theirs, first[-1]) if first else theirs))
            far.append(swap(totals[i][2 * own :], 2))
        if i > 0:
            there = once(far[i - 1], totals[i]) if i < count else far[i - 1]
            first.append(add_up(totals[i - 1][own : 2 * own], there[own:]))
    near = [swap(f, 1) for f in first]
    return [add_up(t[:own], f[:own], n) for t, f, n in zip(totals, far, near)], first[-1]


def once(value, *others):
    return lax.optimization_barrier((value, others))[0]


def add_up(*terms):
    return sum(t.astype(F32) for t in terms).astype(BF16)


def add_pair(total, axis, distance, *others):
    route = [(i, i ^ distance) for i in range(lax.axis_size(axis))]
    mine = total.astype(BF16)
    theirs = lax.ppermute(mine, axis, route)
    return mine.astype(F32) + (once(theirs, *others) if others else theirs).astype(F32)


def step_rows(depth, count):
    step = 512 if count > 1 else 1024
    while depth % step:
        step //= 2
    return step


def stream_weights(w_refs, w_buf, w_sem, start, step, steps, compute):
    count = len(w_refs)

    def copy(k, m):
        slot = lax.rem(k, SLOTS)
        rows = pl.ds(start + k * step, step)
        return pltpu.make_async_copy(w_refs[m].at[rows, :], w_buf.at[slot, m], w_sem.at[slot, m])

    for k in range(min(SLOTS - 1, steps)):
        for m in range(count):
            copy(k, m).start()

    def body(k, carry):
        @pl.when(k + SLOTS - 1 < steps)
        def _():
            for m in range(count):
                copy(k + SLOTS - 1, m).start()

        for m in range(count):
            copy(k, m).wait()
        compute(k, lax.rem(k, SLOTS))
        return carry

    return lambda: lax.fori_loop(0, steps, body, 0)


def weight_scratch(count, step, group):
    return [pltpu.VMEM((SLOTS, count, step, group), BF16), pltpu.SemaphoreType.DMA((SLOTS, count))]


def matmul_cost(rows, depth, group, count):
    return pl.CostEstimate(
        flops=2 * count * rows * depth * group, bytes_accessed=2 * count * depth * group, transcendentals=0
    )


VMEM = pl.BlockSpec(memory_space=pltpu.VMEM)
ANYWHERE = pl.BlockSpec(memory_space=pl.ANY)


def project(pieces, weights, chunk, acc, tp, paired, out_grad, taps, finish):
    rows = sum(p.shape[0] for p in pieces)
    count = len(weights)
    group = weights[0].shape[1]
    start, depth = chunk[0], chunk[1] - chunk[0]
    step = step_rows(depth, count)
    own = rows // tp
    n_x = len(pieces)
    has_acc = acc is not None
    pair = count == 2

    def kernel(*refs):
        x_refs, w_refs, refs = refs[:n_x], refs[n_x : n_x + count], refs[n_x + count :]
        if has_acc:
            acc_refs, refs = refs[:count], refs[count:]
        if finish:
            if not pair:
                grad_ref, refs = refs[0], refs[1:]
            outs, made_ref, edge_ref, totals = refs[:count], refs[count], refs[count + 1], refs[count + 2 : 2 * count + 2]
        else:
            totals = refs[:count]
        x_buf, w_buf, w_sem = refs[-3:]

        def compute(k, slot):
            x = x_buf[:, pl.ds(pl.multiple_of(k * step, step), step)]
            for m in range(count):
                totals[m][...] += jnp.dot(x, w_buf[slot, m], preferred_element_type=F32)

        run = stream_weights(w_refs, w_buf, w_sem, start, step, depth // step, compute)
        at = 0
        for piece in x_refs:
            x_buf[at : at + piece.shape[0], :] = piece[...]
            at += piece.shape[0]
        for m in range(count):
            totals[m][...] = acc_refs[m][...] if has_acc else jnp.zeros_like(totals[m])
        run()
        if finish:
            for b, index in enumerate(row_order(tp, paired)):
                here = block_rows(index, own)
                part = [total[b * own : (b + 1) * own, :].astype(BF16) for total in totals]
                for out, value in zip(outs, part):
                    out[here, :] = value
                other = part[1] if pair else grad_ref[here, :]
                made_ref[here, :] = (part[0].astype(F32) * other.astype(F32)).astype(BF16)
            edge_ref[...] = made_ref[rows - taps :, :] if pair else made_ref[:taps, :]

    in_specs = [VMEM] * n_x + [ANYWHERE] * count
    args = [*pieces, *weights]
    if has_acc:
        in_specs += [VMEM] * count
        args += acc
    totals = (rows, group)
    scratch = [pltpu.VMEM((rows, depth), BF16), *weight_scratch(count, step, group)]
    full = jax.ShapeDtypeStruct((rows, group), BF16)
    if finish:
        if not pair:
            in_specs.append(VMEM)
            args.append(out_grad)
        out_shape = [full] * (count + 1) + [jax.ShapeDtypeStruct((taps, group), BF16)]
        scratch = [pltpu.VMEM(totals, F32)] * count + scratch
    else:
        out_shape = [jax.ShapeDtypeStruct(totals, F32)] * count
    return pl.pallas_call(
        kernel,
        in_specs=in_specs,
        out_specs=[VMEM] * len(out_shape),
        out_shape=out_shape,
        scratch_shapes=scratch,
        compiler_params=pltpu.CompilerParams(vmem_limit_bytes=FWD_VMEM),
        cost_estimate=matmul_cost(rows, depth, group, count),
        name="project",
    )(*args)


LANES = 128


def constant(matrix):
    stacked = np.concatenate(np.split(matrix, matrix.shape[1] // LANES, axis=1), axis=0)
    high = stacked.astype(jnp.bfloat16)
    low = (stacked - high.astype(np.float64)).astype(jnp.bfloat16)
    return jnp.asarray(high), jnp.asarray(low)


def transforms(length, taps):
    size = length + taps
    angle = 2 * np.pi / size * np.outer(np.arange(size // 2) + 0.5, np.arange(size))
    there = np.concatenate([np.cos(angle), -np.sin(angle)], axis=0)
    back = there.T * (2.0 / size)
    lags = back[np.arange(taps, 0, -1)]
    return [*constant(there), *constant(np.concatenate([back[taps:], back[:length], lags], axis=0))]


def window_of(mats):
    return math.isqrt(mats[0].shape[0] * mats[0].shape[1])


def part_of(ref, size, rows, cols):
    height = ref.shape[0] // (size // LANES)
    blocks = range(cols[0] // LANES, cols[1] // LANES)
    return jnp.concatenate([ref[b * height + rows[0] : b * height + rows[1], :] for b in blocks], axis=1)


def dot_there(mats, x, start):
    size = window_of(mats)
    cols = (start, start + x.shape[0])
    y = jnp.dot(part_of(mats[0], size, (0, size), cols), x, preferred_element_type=F32)
    if EXACT:
        y = y + jnp.dot(part_of(mats[1], size, (0, size), cols), x, preferred_element_type=F32)
    return y


def dot_back(mats, rows, re, im):
    y = jnp.concatenate([re, im], axis=0)
    size = y.shape[0]
    high = y.astype(BF16)
    back = part_of(mats[2], size, rows, (0, size))
    out = jnp.dot(back, high, preferred_element_type=F32)
    if EXACT:
        low = (y - high.astype(F32)).astype(BF16)
        out = out + jnp.dot(back, low, preferred_element_type=F32)
        out = out + jnp.dot(part_of(mats[3], size, rows, (0, size)), high, preferred_element_type=F32)
    return out


def by_columns(kernel, mats, arrays, out_shape, scratch, flops, name):
    group = arrays[0].shape[1]
    width = min(256, group)

    def cols(a):
        return pl.BlockSpec((a.shape[0], width), lambda i: (0, i))

    def body(*refs):
        kernel(refs[: len(mats)], *refs[len(mats) :])

    return pl.pallas_call(
        body,
        grid=(group // width,),
        in_specs=[pl.BlockSpec(m.shape, lambda i: (0, 0)) for m in mats] + [cols(a) for a in arrays],
        out_specs=[cols(a) for a in out_shape],
        out_shape=out_shape,
        scratch_shapes=[pltpu.VMEM((rows, width), BF16) for rows in scratch],
        compiler_params=pltpu.CompilerParams(vmem_limit_bytes=MID_VMEM),
        cost_estimate=pl.CostEstimate(
            flops=int(flops * group),
            bytes_accessed=sum(a.size * a.dtype.itemsize for a in [*arrays, *out_shape]),
            transcendentals=0,
        ),
        name=name,
    )(*mats, *arrays)


def transform_taps(filter_taps, mats):
    taps, group = filter_taps.shape
    size = window_of(mats)

    def kernel(mat_refs, taps_ref, out_ref):
        f = taps_ref[...]
        high = f.astype(BF16)
        out = dot_there(mat_refs, high, 0)
        if EXACT:
            low = (f - high.astype(F32)).astype(BF16)
            out = out + jnp.dot(part_of(mat_refs[0], size, (0, size), (0, taps)), low, preferred_element_type=F32)
        out_ref[...] = out

    out = [jax.ShapeDtypeStruct((size, group), F32)]
    return by_columns(kernel, mats[:2], [filter_taps], out, [], 6 * size * taps, "taps")[0]


def transform_rows(product, conv_in_grad, mats, taps):
    length, group = product.shape
    size = window_of(mats)

    def kernel(mat_refs, p_ref, c_ref, p_out, c_out):
        p_out[...] = dot_there(mat_refs, p_ref[...], taps)
        c_out[...] = dot_there(mat_refs, c_ref[...], 0)

    out = [jax.ShapeDtypeStruct((size, group), F32)] * 2
    return by_columns(kernel, mats[:2], [product, conv_in_grad], out, [], 8 * size * length, "transform")


def in_row_order(out_ref, scratch, own, tp, paired):
    for b, index in enumerate(row_order(tp, paired)):
        out_ref[b * own : (b + 1) * own, :] = scratch[block_rows(index, own), :]


def filter_forward(spectra, before, query, out_grad, mats, tp, paired):
    length, group = query.shape
    taps = before.shape[0]
    half = (length + taps) // 2

    def kernel(mat_refs, p_ref, c_ref, h_ref, before_ref, q_ref, grad_ref, mixed_ref, qg_ref, fg_ref, sq):
        p = p_ref[...] + dot_there(mat_refs, before_ref[...], 0)
        pr, pi, hr, hi = p[:half], p[half:], h_ref[:half, :], h_ref[half:, :]
        conv = dot_back(mat_refs, (0, length), pr * hr - pi * hi, pr * hi + pi * hr)
        mixed_ref[...] = (q_ref[...].astype(F32) * conv).astype(BF16)
        sq[...] = (grad_ref[...].astype(F32) * conv).astype(BF16)
        in_row_order(qg_ref, sq, length // tp, tp, paired)
        cr, ci = c_ref[:half, :], c_ref[half:, :]
        lags = (2 * length, 2 * length + taps)
        fg_ref[...] = dot_back(mat_refs, lags, cr * pr + ci * pi, cr * pi - ci * pr).astype(BF16)

    full = jax.ShapeDtypeStruct((length, group), BF16)
    out = [full, full, jax.ShapeDtypeStruct((taps, group), BF16)]
    flops = 2 * half * 2 * (2 * taps + 3 * (length + taps))
    return by_columns(kernel, mats, [*spectra, before, query, out_grad], out, [length], flops, "conv")


def filter_backward(spectra, after, keys, values, mats, tp, paired):
    length, group = keys.shape
    taps = after.shape[0]
    half = (length + taps) // 2

    def kernel(mat_refs, c_ref, h_ref, after_ref, k_ref, v_ref, kg_ref, vg_ref, sk, sv):
        g = c_ref[...] + dot_there(mat_refs, after_ref[...], length)
        gr, gi, hr, hi = g[:half], g[half:], h_ref[:half, :], h_ref[half:, :]
        product_grad = dot_back(mat_refs, (length, 2 * length), hr * gr + hi * gi, hr * gi - hi * gr)
        sk[...] = (product_grad * v_ref[...].astype(F32)).astype(BF16)
        sv[...] = (product_grad * k_ref[...].astype(F32)).astype(BF16)
        in_row_order(kg_ref, sk, length // tp, tp, paired)
        in_row_order(vg_ref, sv, length // tp, tp, paired)

    out = [jax.ShapeDtypeStruct((length, group), BF16)] * 2
    flops = 2 * half * 2 * (2 * taps + 3 * length)
    return by_columns(kernel, mats, [*spectra, after, keys, values], out, [length, length], flops, "conv_back")


def project_back(grads, weights, chunk, acc, parts):
    rows, group = grads[0].shape
    count = len(grads)
    start, depth = chunk[0], chunk[1] - chunk[0]
    step = step_rows(depth, count)
    n_out = max(parts, 1)
    share = rows // n_out
    has_acc = acc is not None

    def kernel(*refs):
        g_refs, w_refs, refs = refs[:count], refs[count : 2 * count], refs[2 * count :]
        if has_acc:
            acc_ref, refs = refs[0], refs[1:]
        out_refs, (w_buf, w_sem) = refs[:n_out], refs[n_out:]

        def compute(k, slot):
            at = pl.ds(pl.multiple_of(k * step, step), step)
            total = acc_ref[:, at] if has_acc else None
            for m in range(count):
                term = lax.dot_general(
                    g_refs[m][...], w_buf[slot, m], (((1,), (1,)), ((), ())), preferred_element_type=F32
                )
                total = term if total is None else total + term
            for i in range(n_out):
                out_refs[i][:, at] = total[i * share : (i + 1) * share].astype(out_refs[i].dtype)

        stream_weights(w_refs, w_buf, w_sem, start, step, depth // step, compute)()

    args = [*grads, *weights] + ([acc] if has_acc else [])
    return pl.pallas_call(
        kernel,
        in_specs=[VMEM] * count + [ANYWHERE] * count + [VMEM] * has_acc,
        out_specs=[VMEM] * n_out,
        out_shape=[jax.ShapeDtypeStruct((share, depth), BF16 if parts else F32)] * n_out,
        scratch_shapes=weight_scratch(count, step, group),
        compiler_params=pltpu.CompilerParams(vmem_limit_bytes=BWD_VMEM),
        cost_estimate=matmul_cost(rows, depth, group, count),
        name="project_back",
    )(*args)


def on_device(inputs, query_weight, key_weight, value_weight, filter_taps, out_grad):
    tp = lax.axis_size("tp")
    paired = tp == 8
    own_rows, width = inputs.shape
    taps = filter_taps.shape[0]
    mats = transforms(own_rows * tp, taps)
    h = transform_taps(filter_taps, mats)
    chunks = bounds(width, FWD_PARTS)
    gathered = gather_rows(inputs, chunks, paired)
    pair = (key_weight, value_weight)
    acc = [None] * 3
    for pieces, chunk in zip(gathered[:-1], chunks[:-1]):
        pieces[0] = once(pieces[0], h)
        acc = project(
            pieces, (query_weight, *pair), chunk, None if acc[0] is None else acc, tp, paired, None, taps, False
        )
    keys, values, product, tail = project(
        gathered[-1], pair, chunks[-1], acc[1:], tp, paired, None, taps, True
    )
    before = from_behind(tail, "ctx", 1)
    query, conv_in_grad, head = project(
        gathered[-1], (query_weight,), chunks[-1], [once(acc[0], product)], tp, paired, out_grad, taps, True
    )
    after = from_behind(head, "ctx", -1)
    p, c = transform_rows(product, conv_in_grad, mats, taps)
    mixed, query_grad, local_taps = filter_forward((p, c, h), before, query, out_grad, mats, tp, paired)
    chunks = bounds(width, BWD_PARTS)
    partial = project_back((query_grad,), (query_weight,), chunks[0], None, 0)[0]
    keys_grad, values_grad = filter_backward((c, h), once(after, partial), keys, values, mats, tp, paired)
    size = lax.axis_size("ctx")
    distances = [2**i for i in range(size.bit_length() - 1)] if size & (size - 1) == 0 else []
    pieces, totals = [], []
    for i, chunk in enumerate(chunks):
        if i == 0:
            pieces.append(project_back((keys_grad, values_grad), pair, chunk, partial, 2 if paired else 1))
            continue
        ready = [pieces[-1][0]]
        if len(distances) > 1:
            local_taps = add_pair(local_taps, "ctx", distances.pop(0))
            ready.append(local_taps)
        if paired and i > 1:
            totals.append(add_up(pieces[i - 2][0], swap(pieces[i - 2][1], 0)))
            ready.append(totals[-1])
        grads = (once(query_grad, *ready), keys_grad, values_grad)
        pieces.append(project_back(grads, (query_weight, *pair), chunk, None, 2 if paired else 1))
    if paired:
        summed, last = scatter_rows(pieces, totals, own_rows)
    else:
        summed = [lax.psum_scatter(p, "tp", scatter_dimension=0, tiled=True) for (p,) in pieces]
        last = summed[-1]
    if distances:
        for distance in distances:
            local_taps = add_pair(local_taps, "ctx", distance, last)
    else:
        local_taps = lax.psum(local_taps, "ctx").astype(F32)
    return mixed, jnp.concatenate(summed, axis=1), local_taps


def solution(mesh):
    in_specs = (
        P(("ctx", "tp"), None),
        P(None, "tp"),
        P(None, "tp"),
        P(None, "tp"),
        P(None, "tp"),
        P("ctx", "tp"),
    )
    out_specs = (P("ctx", "tp"), P(("ctx", "tp"), None), P(None, "tp"))
    return jax.shard_map(
        on_device, mesh=mesh, in_specs=in_specs, out_specs=out_specs, check_vma=False
    )
```

```python
import math

import jax
import jax.numpy as jnp
import numpy as np
from jax import lax
from jax.experimental import pallas as pl
from jax.experimental.pallas import tpu as pltpu
from jax.sharding import PartitionSpec as P

F32 = jnp.float32
BF16 = jnp.bfloat16
FWD_VMEM = 42 * 2**20
BWD_VMEM = 42 * 2**20
MIX_VMEM = 35 * 2**20
MID_VMEM = 24 * 2**20
FWD_PARTS = (2, 6)
BWD_PARTS = (4, 3, 1)


def bounds(width, parts):
    edges = np.cumsum((0,) + parts) * width // sum(parts)
    return [(int(a), int(b)) for a, b in zip(edges[:-1], edges[1:])]


def from_behind(block, axis, distance):
    devices = range(lax.axis_size(axis))
    route = [(i - distance, i) for i in devices if i - distance in devices]
    return lax.ppermute(block, axis, route)


def swap(block, way):
    offsets = {0: (1, 1), 1: (2, 4), 2: (4, 2)}[way]
    return lax.ppermute(block, "tp", [(i, i ^ offsets[i % 2]) for i in range(8)])


def row_order(tp, paired):
    if not paired:
        return list(range(tp))
    me = lax.axis_index("tp")
    first = 2 + 2 * (me % 2)
    second = 6 - first
    own = [me, me ^ first, me ^ second, me ^ 6]
    other = me ^ 1
    return own + [other, other ^ second, other ^ first, other ^ 6]


def block_rows(index, own):
    start = index * own
    return pl.ds(start if isinstance(start, int) else pl.multiple_of(start, own), own)


def once(value, *others):
    return lax.optimization_barrier((value, others))[0]


def add_up(*terms):
    return sum(t.astype(F32) for t in terms).astype(BF16)


def add_pair(total, axis, distance, *others):
    route = [(i, i ^ distance) for i in range(lax.axis_size(axis))]
    mine = total.astype(BF16)
    theirs = lax.ppermute(mine, axis, route)
    return mine.astype(F32) + (once(theirs, *others) if others else theirs).astype(F32)


def gather_rows(block, chunks, paired, *others):
    if not paired:
        return [[lax.all_gather(block[:, a:b], "tp", axis=0, tiled=True)] for a, b in chunks]
    first, pieces = once(swap(block, 1), *others), []
    for a, b in chunks:
        near = jnp.concatenate([block[:, a:b], first[:, a:b]], axis=0)
        pieces.append([near, swap(near, 2), swap(near, 0)])
    return pieces


def scatter_rows(pieces, totals, own):
    far, first, count = [], [], len(pieces)
    for i in range(count + 1):
        if i < count:
            if i >= len(totals):
                totals.append(chip_sums(pieces[i], own, first[-1:]))
            far.append(swap(totals[i][1], 2))
        if i > 0:
            there = once(far[i - 1], totals[i][1]) if i < count else far[i - 1]
            first.append(add_up(totals[i - 1][0][own:], there[own:]))
    near = [swap(f, 1) for f in first]
    return [add_up(t[:own], f[:own], n) for (t, _), f, n in zip(totals, far, near)], first


def chip_sums(piece, own, others=()):
    keep, give = piece
    theirs = swap(give, 0)
    if others:
        theirs = once(theirs, *others)
    far = add_up(keep[2 * own :], theirs[2 * own :])
    return add_up(keep[: 2 * own], theirs[: 2 * own]), far


def step_rows(depth, count):
    step = 512 if count > 1 else 1024
    while depth % step:
        step //= 2
    return step


def stream_weights(w_refs, w_buf, w_sem, start, steps, compute):
    count = len(w_refs)
    slots, _, step, _ = w_buf.shape
    ahead = min(slots - 1, steps)

    def copy(k, m):
        slot = lax.rem(k, slots)
        rows = pl.ds(start + k * step, step)
        return pltpu.make_async_copy(w_refs[m].at[rows, :], w_buf.at[slot, m], w_sem.at[slot, m])

    for k in range(ahead):
        for m in range(count):
            copy(k, m).start()

    def body(k, carry):
        @pl.when(k + ahead < steps)
        def _():
            for m in range(count):
                copy(k + ahead, m).start()

        for m in range(count):
            copy(k, m).wait()
        compute(k, lax.rem(k, slots))
        return carry

    return lambda: lax.fori_loop(0, steps, body, 0)


def weight_scratch(count, step, group, slots=3):
    return [pltpu.VMEM((slots, count, step, group), BF16), pltpu.SemaphoreType.DMA((slots, count))]


def contract(left, right):
    return lax.dot_general(left, right, (((1,), (1,)), ((), ())), preferred_element_type=F32)


def matmul_cost(rows, depth, group, count):
    return pl.CostEstimate(
        flops=2 * count * rows * depth * group, bytes_accessed=2 * count * depth * group, transcendentals=0
    )


VMEM = pl.BlockSpec(memory_space=pltpu.VMEM)
ANYWHERE = pl.BlockSpec(memory_space=pl.ANY)


def project(pieces, weights, chunk, acc, tp, paired, taps, finish, out_grad=None, product=None, mats=()):
    rows = sum(p.shape[0] for p in pieces)
    count = len(weights)
    group = weights[0].shape[1]
    start, depth = chunk[0], chunk[1] - chunk[0]
    step = step_rows(depth, count)
    own = rows // tp
    n_x = len(pieces)
    has_acc = acc is not None
    pair = count == 2

    def kernel(*refs):
        x_refs, w_refs, refs = refs[:n_x], refs[n_x : n_x + count], refs[n_x + count :]
        if has_acc:
            acc_refs, refs = refs[:count], refs[count:]
        if finish:
            if not pair:
                grad_ref, prod_ref, mat_refs, refs = refs[0], refs[1], refs[2 : 2 + len(mats)], refs[2 + len(mats) :]
            outs, made_ref, edge_ref, refs = refs[:count], refs[count], refs[count + 1], refs[count + 2 :]
            if not pair:
                spectrum_ref, refs = refs[0], refs[1:]
            totals = refs[:count]
        else:
            totals = refs[:count]
        x_buf, w_buf, w_sem = refs[-3:]

        def compute(k, slot):
            x = x_buf[:, pl.ds(pl.multiple_of(k * step, step), step)]
            for m in range(count):
                totals[m][...] += jnp.dot(x, w_buf[slot, m], preferred_element_type=F32)

        run = stream_weights(w_refs, w_buf, w_sem, start, depth // step, compute)
        at = 0
        for piece in x_refs:
            x_buf[at : at + piece.shape[0], :] = piece[...]
            at += piece.shape[0]
        for m in range(count):
            totals[m][...] = acc_refs[m][...] if has_acc else jnp.zeros_like(totals[m])
        if finish and not pair:
            for cols in column_blocks(group):
                spectrum_ref[:, cols] = dot_there(mat_refs, prod_ref[:, cols], taps)
        run()
        if finish:
            for b, index in enumerate(row_order(tp, paired)):
                here = block_rows(index, own)
                part = [total[b * own : (b + 1) * own, :].astype(BF16) for total in totals]
                for out, value in zip(outs, part):
                    out[here, :] = value
                other = part[1] if pair else grad_ref[here, :]
                made_ref[here, :] = (part[0].astype(F32) * other.astype(F32)).astype(BF16)
            edge_ref[...] = made_ref[rows - taps :, :] if pair else made_ref[:taps, :]

    in_specs = [VMEM] * n_x + [ANYWHERE] * count
    args = [*pieces, *weights]
    if has_acc:
        in_specs += [VMEM] * count
        args += acc
    totals = (rows, group)
    scratch = [pltpu.VMEM((rows, depth), BF16), *weight_scratch(count, step, group)]
    full = jax.ShapeDtypeStruct((rows, group), BF16)
    if finish:
        if not pair:
            in_specs += [VMEM] * (2 + len(mats))
            args += [out_grad, product, *mats]
        out_shape = [full] * (count + 1) + [jax.ShapeDtypeStruct((taps, group), BF16)]
        if not pair:
            out_shape.append(jax.ShapeDtypeStruct((rows + taps, group), F32))
        scratch = [pltpu.VMEM(totals, F32)] * count + scratch
    else:
        out_shape = [jax.ShapeDtypeStruct(totals, F32)] * count
    return pl.pallas_call(
        kernel,
        in_specs=in_specs,
        out_specs=[VMEM] * len(out_shape),
        out_shape=out_shape,
        scratch_shapes=scratch,
        compiler_params=pltpu.CompilerParams(vmem_limit_bytes=FWD_VMEM),
        cost_estimate=matmul_cost(rows, depth, group, count),
        name="project",
    )(*args)


LANES = 128


def constant(matrix):
    stacked = np.concatenate(np.split(matrix, matrix.shape[1] // LANES, axis=1), axis=0)
    high = stacked.astype(jnp.bfloat16)
    low = (stacked - high.astype(np.float64)).astype(jnp.bfloat16)
    return jnp.asarray(high), jnp.asarray(low)


def transforms(length, taps):
    size = length + taps
    angle = 2 * np.pi / size * np.outer(np.arange(size // 2) + 0.5, np.arange(size))
    there = np.concatenate([np.cos(angle), -np.sin(angle)], axis=0)
    back = there.T * (2.0 / size)
    lags = back[np.arange(taps, 0, -1)]
    return [*constant(there), constant(np.concatenate([back[taps:], back[:length], lags], axis=0))[0]]


def window_of(mats):
    return math.isqrt(mats[0].shape[0] * mats[0].shape[1])


def part_of(ref, size, rows, cols):
    height = ref.shape[0] // (size // LANES)
    blocks = range(cols[0] // LANES, cols[1] // LANES)
    return jnp.concatenate([ref[b * height + rows[0] : b * height + rows[1], :] for b in blocks], axis=1)


def dot_there(mats, x, start):
    size = window_of(mats)
    cols = (start, start + x.shape[0])
    return jnp.dot(part_of(mats[0], size, (0, size), cols), x, preferred_element_type=F32)


def dot_back(mats, rows, re, im):
    y = jnp.concatenate([re, im], axis=0).astype(BF16)
    size = y.shape[0]
    return jnp.dot(part_of(mats[1], size, rows, (0, size)), y, preferred_element_type=F32)


def column_blocks(group):
    width = min(256, group)
    return [slice(a, a + width) for a in range(0, group, width)]


def transform_taps(filter_taps, there):
    taps, group = filter_taps.shape
    size = window_of(there)

    def kernel(high_ref, low_ref, taps_ref, out_ref):
        cols = ((0, size), (0, taps))
        high, low = part_of(high_ref, size, *cols), part_of(low_ref, size, *cols)
        f = taps_ref[...]
        f_high = f.astype(BF16)
        f_low = (f - f_high.astype(F32)).astype(BF16)
        out = jnp.dot(high, f_low, preferred_element_type=F32) + jnp.dot(low, f_high, preferred_element_type=F32)
        out_ref[...] = out + jnp.dot(high, f_high, preferred_element_type=F32)

    return pl.pallas_call(
        kernel,
        in_specs=[VMEM] * 3,
        out_specs=VMEM,
        out_shape=jax.ShapeDtypeStruct((size, group), F32),
        compiler_params=pltpu.CompilerParams(vmem_limit_bytes=MID_VMEM),
        cost_estimate=pl.CostEstimate(flops=6 * size * taps * group, bytes_accessed=4 * size * group, transcendentals=0),
        name="taps",
    )(*there, filter_taps)


def in_row_order(out_ref, scratch, own, tp, paired):
    for b, index in enumerate(row_order(tp, paired)):
        out_ref[b * own : (b + 1) * own, :] = scratch[block_rows(index, own), :]


def filter_forward(spectra, before, query, conv_in_grad, out_grad, mats, weight, chunk, tp, paired):
    length, group = query.shape
    taps = before.shape[0]
    half = (length + taps) // 2
    start, depth = chunk[0], chunk[1] - chunk[0]
    step = step_rows(depth, 1)

    def kernel(there, back, p_ref, h_ref, before_ref, q_ref, cig_ref, grad_ref, w_ref, mixed_ref, qg_ref, fg_ref, c_ref,
               total_ref, sq, w_buf, w_sem):
        def compute(k, slot):
            at = pl.ds(pl.multiple_of(k * step, step), step)
            total_ref[:, at] = contract(qg_ref[...], w_buf[slot, 0])

        run = stream_weights([w_ref], w_buf, w_sem, start, depth // step, compute)
        mat_refs = (there, back)
        for cols in column_blocks(group):
            p = p_ref[:, cols] + dot_there(mat_refs, before_ref[:, cols], 0)
            c = dot_there(mat_refs, cig_ref[:, cols], 0)
            c_ref[:, cols] = c
            h = h_ref[:, cols]
            pr, pi, cr, ci, hr, hi = p[:half], p[half:], c[:half], c[half:], h[:half], h[half:]
            conv = dot_back(mat_refs, (0, length), pr * hr - pi * hi, pr * hi + pi * hr)
            mixed_ref[:, cols] = (q_ref[:, cols].astype(F32) * conv).astype(BF16)
            sq[:, cols] = (grad_ref[:, cols].astype(F32) * conv).astype(BF16)
            lags = (2 * length, 2 * length + taps)
            fg_ref[:, cols] = dot_back(mat_refs, lags, cr * pr + ci * pi, cr * pi - ci * pr).astype(BF16)
        in_row_order(qg_ref, sq, length // tp, tp, paired)
        run()

    full = jax.ShapeDtypeStruct((length, group), BF16)
    out_shape = [
        full,
        full,
        jax.ShapeDtypeStruct((taps, group), BF16),
        jax.ShapeDtypeStruct((length + taps, group), F32),
        jax.ShapeDtypeStruct((length, depth), F32),
    ]
    return pl.pallas_call(
        kernel,
        in_specs=[VMEM] * 8 + [ANYWHERE],
        out_specs=[VMEM] * 5,
        out_shape=out_shape,
        scratch_shapes=[pltpu.VMEM((length, group), BF16), *weight_scratch(1, step, group, 5)],
        compiler_params=pltpu.CompilerParams(vmem_limit_bytes=MIX_VMEM),
        cost_estimate=matmul_cost(length, depth + 2048, group, 1),
        name="conv",
    )(*mats, *spectra, before, query, conv_in_grad, out_grad, weight)


def filter_backward(spectra, after, keys, values, mats, weights, chunk, partial, tp, paired):
    length, group = keys.shape
    taps = after.shape[0]
    half = (length + taps) // 2
    start, depth = chunk[0], chunk[1] - chunk[0]
    step = step_rows(depth, 2)
    parts = 2 if paired else 1
    share = length // parts

    def kernel(*refs):
        there, back, c_ref, h_ref, after_ref, k_ref, v_ref, partial_ref, *refs = refs
        w_refs, out_refs, (kg_ref, vg_ref, sk, sv, w_buf, w_sem) = refs[:2], refs[2 : 2 + parts], refs[2 + parts :]

        def compute(k, slot):
            at = pl.ds(pl.multiple_of(k * step, step), step)
            total = partial_ref[:, at] + contract(kg_ref[...], w_buf[slot, 0]) + contract(vg_ref[...], w_buf[slot, 1])
            for i in range(parts):
                out_refs[i][:, at] = total[i * share : (i + 1) * share].astype(BF16)

        run = stream_weights(w_refs, w_buf, w_sem, start, depth // step, compute)
        mat_refs = (there, back)
        for cols in column_blocks(group):
            g = c_ref[:, cols] + dot_there(mat_refs, after_ref[:, cols], length)
            h = h_ref[:, cols]
            gr, gi, hr, hi = g[:half], g[half:], h[:half], h[half:]
            product_grad = dot_back(mat_refs, (length, 2 * length), hr * gr + hi * gi, hr * gi - hi * gr)
            sk[:, cols] = (product_grad * v_ref[:, cols].astype(F32)).astype(BF16)
            sv[:, cols] = (product_grad * k_ref[:, cols].astype(F32)).astype(BF16)
        in_row_order(kg_ref, sk, length // tp, tp, paired)
        in_row_order(vg_ref, sv, length // tp, tp, paired)
        run()

    full = jax.ShapeDtypeStruct((length, group), BF16)
    return pl.pallas_call(
        kernel,
        in_specs=[VMEM] * 8 + [ANYWHERE] * 2,
        out_specs=[VMEM] * (parts + 2),
        out_shape=[jax.ShapeDtypeStruct((share, depth), BF16)] * parts + [full] * 2,
        scratch_shapes=[pltpu.VMEM((length, group), BF16)] * 2 + weight_scratch(2, step, group, 5),
        compiler_params=pltpu.CompilerParams(vmem_limit_bytes=MIX_VMEM),
        cost_estimate=matmul_cost(length, depth + 1024, group, 2),
        name="conv_back",
    )(*mats, *spectra, after, keys, values, partial, *weights)


def project_back(grads, weights, chunk, parts, ready):
    rows, group = grads[0].shape
    count = len(grads)
    start, depth = chunk[0], chunk[1] - chunk[0]
    step = step_rows(depth, count)
    share = rows // parts
    n_in = 2 * count + len(ready)

    def kernel(*refs):
        g_refs, w_refs = refs[:count], refs[count : 2 * count]
        out_refs, (w_buf, w_sem) = refs[n_in : n_in + parts], refs[n_in + parts :]

        def compute(k, slot):
            at = pl.ds(pl.multiple_of(k * step, step), step)
            total = contract(g_refs[0][...], w_buf[slot, 0])
            for m in range(1, count):
                total = total + contract(g_refs[m][...], w_buf[slot, m])
            for i in range(parts):
                out_refs[i][:, at] = total[i * share : (i + 1) * share].astype(BF16)

        stream_weights(w_refs, w_buf, w_sem, start, depth // step, compute)()

    return pl.pallas_call(
        kernel,
        in_specs=[VMEM] * count + [ANYWHERE] * count + [VMEM] * len(ready),
        out_specs=[VMEM] * parts,
        out_shape=[jax.ShapeDtypeStruct((share, depth), BF16)] * parts,
        scratch_shapes=weight_scratch(count, step, group),
        compiler_params=pltpu.CompilerParams(vmem_limit_bytes=BWD_VMEM),
        cost_estimate=matmul_cost(rows, depth, group, count),
        name="project_back",
    )(*grads, *weights, *ready)


def on_device(inputs, query_weight, key_weight, value_weight, filter_taps, out_grad):
    tp = lax.axis_size("tp")
    paired = tp == 8
    own_rows, width = inputs.shape
    taps = filter_taps.shape[0]
    there, there_low, back = transforms(own_rows * tp, taps)
    mats = (there, back)
    h = transform_taps(filter_taps, (there, there_low))
    chunks = bounds(width, FWD_PARTS)
    gathered = gather_rows(inputs, chunks, paired, h)
    pair = (key_weight, value_weight)
    acc = None
    for i, (pieces, chunk) in enumerate(zip(gathered, chunks)):
        if paired:
            if i + 1 < len(chunks):
                pieces[0] = once(pieces[0], gathered[i + 1][0])
            pieces.append(swap(once(pieces[1], acc[0]) if acc else pieces[1], 0))
        if i + 1 < len(chunks):
            acc = project(pieces, (query_weight, *pair), chunk, acc, tp, paired, taps, False)
    keys, values, product, tail = project(pieces, pair, chunk, acc[1:], tp, paired, taps, True)
    before = from_behind(tail, "ctx", 1)
    query, conv_in_grad, head, p = project(
        pieces, (query_weight,), chunk, acc[:1], tp, paired, taps, True, out_grad, product, mats
    )
    after = from_behind(head, "ctx", -1)
    chunks = bounds(width, BWD_PARTS)
    mixed, query_grad, local_taps, c, partial = filter_forward(
        (p, h), before, query, conv_in_grad, out_grad, mats, query_weight, chunks[0], tp, paired
    )
    *piece, keys_grad, values_grad = filter_backward(
        (c, h), after, keys, values, mats, pair, chunks[0], partial, tp, paired
    )
    size = lax.axis_size("ctx")
    distances = [2**i for i in range(size.bit_length() - 1)] if size & (size - 1) == 0 else []
    pieces, totals = [piece], []
    grads, weights = (query_grad, keys_grad, values_grad), (query_weight, *pair)
    for i, chunk in enumerate(chunks[1:]):
        ready = []
        if i == 1 and distances:
            local_taps = add_pair(local_taps, "ctx", distances.pop(0))
            ready.append(local_taps)
        if paired and i > 0:
            totals.append(chip_sums(pieces[i - 1], own_rows))
            ready.append(totals[-1][1])
        pieces.append(project_back(grads, weights, chunk, 2 if paired else 1, ready))
    if paired:
        summed, last = scatter_rows(pieces, totals, own_rows)
    else:
        summed = [lax.psum_scatter(p, "tp", scatter_dimension=0, tiled=True) for (p,) in pieces]
        last = summed
    for distance in distances:
        local_taps = add_pair(local_taps, "ctx", distance, *last)
    if size & (size - 1):
        local_taps = lax.psum(local_taps, "ctx")
    return mixed, jnp.concatenate(summed, axis=1), local_taps.astype(F32)


def solution(mesh):
    in_specs = (
        P(("ctx", "tp"), None),
        P(None, "tp"),
        P(None, "tp"),
        P(None, "tp"),
        P(None, "tp"),
        P("ctx", "tp"),
    )
    out_specs = (P("ctx", "tp"), P(("ctx", "tp"), None), P(None, "tp"))
    return jax.shard_map(
        on_device, mesh=mesh, in_specs=in_specs, out_specs=out_specs, check_vma=False
    )
```

```python
import math

import jax
import jax.numpy as jnp
import numpy as np
from jax import lax
from jax.experimental import pallas as pl
from jax.experimental.pallas import tpu as pltpu
from jax.sharding import PartitionSpec as P

F32 = jnp.float32
BF16 = jnp.bfloat16
FWD_VMEM = 42 * 2**20
BWD_VMEM = 42 * 2**20
MIX_VMEM = 35 * 2**20
MID_VMEM = 24 * 2**20
FWD_PARTS = (2, 6)
BWD_PARTS = (5, 3)


def bounds(width, parts):
    edges = np.cumsum((0,) + parts) * width // sum(parts)
    return [(int(a), int(b)) for a, b in zip(edges[:-1], edges[1:])]


def from_behind(block, axis, distance):
    devices = range(lax.axis_size(axis))
    route = [(i - distance, i) for i in devices if i - distance in devices]
    return lax.ppermute(block, axis, route)


def swap(block, way):
    offsets = {0: (1, 1), 1: (2, 4), 2: (4, 2)}[way]
    return lax.ppermute(block, "tp", [(i, i ^ offsets[i % 2]) for i in range(8)])


def row_order(tp, paired):
    if not paired:
        return list(range(tp))
    me = lax.axis_index("tp")
    first = 2 + 2 * (me % 2)
    second = 6 - first
    own = [me, me ^ first, me ^ second, me ^ 6]
    other = me ^ 1
    return own + [other, other ^ second, other ^ first, other ^ 6]


def block_rows(index, own):
    start = index * own
    return pl.ds(start if isinstance(start, int) else pl.multiple_of(start, own), own)


def once(value, *others):
    return lax.optimization_barrier((value, others))[0]


def add_up(*terms):
    return sum(t.astype(F32) for t in terms).astype(BF16)


def add_pair(total, axis, distance, *others):
    route = [(i, i ^ distance) for i in range(lax.axis_size(axis))]
    mine = total.astype(BF16)
    theirs = lax.ppermute(mine, axis, route)
    return mine.astype(F32) + (once(theirs, *others) if others else theirs).astype(F32)


def gather_rows(block, chunks, paired, *others):
    if not paired:
        return [[lax.all_gather(block[:, a:b], "tp", axis=0, tiled=True)] for a, b in chunks]
    first, pieces = once(swap(block, 1), *others), []
    for a, b in chunks:
        near = jnp.concatenate([block[:, a:b], first[:, a:b]], axis=0)
        pieces.append([near, swap(near, 2), swap(near, 0)])
    return pieces


def scatter_rows(pieces, totals, own):
    far, first = [swap(t[1], 2) for t in totals], []
    first.append(add_up(totals[0][0][own:], far[0][own:]))
    for piece in pieces[1:]:
        totals.append(chip_sums(piece, own, first[-1:]))
        far.append(swap(totals[-1][1], 2))
        first.append(add_up(totals[-1][0][own:], far[-1][own:]))
    near = [swap(f, 1) for f in first]
    return [add_up(t[:own], f[:own], n) for (t, _), f, n in zip(totals, far, near)], first


def chip_sums(piece, own, others=()):
    keep, give = piece
    theirs = swap(give, 0)
    if others:
        theirs = once(theirs, *others)
    far = add_up(keep[2 * own :], theirs[2 * own :])
    return add_up(keep[: 2 * own], theirs[: 2 * own]), far


def step_rows(depth, count):
    step = 512 if count > 1 else 1024
    while depth % step:
        step //= 2
    return step


def stream_weights(w_refs, w_buf, w_sem, start, steps, compute):
    count = len(w_refs)
    slots, _, step, _ = w_buf.shape
    ahead = min(slots - 1, steps)

    def copy(k, m):
        slot = lax.rem(k, slots)
        rows = pl.ds(start + k * step, step)
        return pltpu.make_async_copy(w_refs[m].at[rows, :], w_buf.at[slot, m], w_sem.at[slot, m])

    for k in range(ahead):
        for m in range(count):
            copy(k, m).start()

    def body(k, carry):
        @pl.when(k + ahead < steps)
        def _():
            for m in range(count):
                copy(k + ahead, m).start()

        for m in range(count):
            copy(k, m).wait()
        compute(k, lax.rem(k, slots))
        return carry

    return lambda: lax.fori_loop(0, steps, body, 0)


def weight_scratch(count, step, group, slots=3):
    return [pltpu.VMEM((slots, count, step, group), BF16), pltpu.SemaphoreType.DMA((slots, count))]


def contract(left, right):
    return lax.dot_general(left, right, (((1,), (1,)), ((), ())), preferred_element_type=F32)


def matmul_cost(rows, depth, group, count):
    return pl.CostEstimate(
        flops=2 * count * rows * depth * group, bytes_accessed=2 * count * depth * group, transcendentals=0
    )


VMEM = pl.BlockSpec(memory_space=pltpu.VMEM)
ANYWHERE = pl.BlockSpec(memory_space=pl.ANY)


def project(pieces, weights, chunk, acc, tp, paired, taps, finish, out_grad=None, product=None, mats=()):
    rows = sum(p.shape[0] for p in pieces)
    count = len(weights)
    group = weights[0].shape[1]
    start, depth = chunk[0], chunk[1] - chunk[0]
    step = step_rows(depth, count)
    own = rows // tp
    n_x = len(pieces)
    has_acc = acc is not None
    pair = count == 2

    def kernel(*refs):
        x_refs, w_refs, refs = refs[:n_x], refs[n_x : n_x + count], refs[n_x + count :]
        if has_acc:
            acc_refs, refs = refs[:count], refs[count:]
        if finish:
            if not pair:
                grad_ref, prod_ref, mat_refs, refs = refs[0], refs[1], refs[2 : 2 + len(mats)], refs[2 + len(mats) :]
            outs, made_ref, edge_ref, refs = refs[:count], refs[count], refs[count + 1], refs[count + 2 :]
            if not pair:
                spectrum_ref, refs = refs[0], refs[1:]
            totals = refs[:count]
        else:
            totals = refs[:count]
        x_buf, w_buf, w_sem = refs[-3:]

        def compute(k, slot):
            x = x_buf[:, pl.ds(pl.multiple_of(k * step, step), step)]
            for m in range(count):
                totals[m][...] += jnp.dot(x, w_buf[slot, m], preferred_element_type=F32)

        run = stream_weights(w_refs, w_buf, w_sem, start, depth // step, compute)
        at = 0
        for piece in x_refs:
            x_buf[at : at + piece.shape[0], :] = piece[...]
            at += piece.shape[0]
        for m in range(count):
            totals[m][...] = acc_refs[m][...] if has_acc else jnp.zeros_like(totals[m])
        if finish and not pair:
            for cols in column_blocks(group):
                spectrum_ref[:, cols] = dot_there(mat_refs, prod_ref[:, cols], taps)
        run()
        if finish:
            for b, index in enumerate(row_order(tp, paired)):
                here = block_rows(index, own)
                part = [total[b * own : (b + 1) * own, :].astype(BF16) for total in totals]
                for out, value in zip(outs, part):
                    out[here, :] = value
                other = part[1] if pair else grad_ref[here, :]
                made_ref[here, :] = (part[0].astype(F32) * other.astype(F32)).astype(BF16)
            edge_ref[...] = made_ref[rows - taps :, :] if pair else made_ref[:taps, :]

    in_specs = [VMEM] * n_x + [ANYWHERE] * count
    args = [*pieces, *weights]
    if has_acc:
        in_specs += [VMEM] * count
        args += acc
    totals = (rows, group)
    scratch = [pltpu.VMEM((rows, depth), BF16), *weight_scratch(count, step, group)]
    full = jax.ShapeDtypeStruct((rows, group), BF16)
    if finish:
        if not pair:
            in_specs += [VMEM] * (2 + len(mats))
            args += [out_grad, product, *mats]
        out_shape = [full] * (count + 1) + [jax.ShapeDtypeStruct((taps, group), BF16)]
        if not pair:
            out_shape.append(jax.ShapeDtypeStruct((rows + taps, group), F32))
        scratch = [pltpu.VMEM(totals, F32)] * count + scratch
    else:
        out_shape = [jax.ShapeDtypeStruct(totals, F32)] * count
    return pl.pallas_call(
        kernel,
        in_specs=in_specs,
        out_specs=[VMEM] * len(out_shape),
        out_shape=out_shape,
        scratch_shapes=scratch,
        compiler_params=pltpu.CompilerParams(vmem_limit_bytes=FWD_VMEM),
        cost_estimate=matmul_cost(rows, depth, group, count),
        name="project",
    )(*args)


LANES = 128


def constant(matrix):
    stacked = np.concatenate(np.split(matrix, matrix.shape[1] // LANES, axis=1), axis=0)
    high = stacked.astype(jnp.bfloat16)
    low = (stacked - high.astype(np.float64)).astype(jnp.bfloat16)
    return jnp.asarray(high), jnp.asarray(low)


def transforms(length, taps):
    size = length + taps
    angle = 2 * np.pi / size * np.outer(np.arange(size // 2) + 0.5, np.arange(size))
    there = np.concatenate([np.cos(angle), -np.sin(angle)], axis=0)
    back = there.T * (2.0 / size)
    lags = back[np.arange(taps, 0, -1)]
    return [*constant(there), constant(np.concatenate([back[taps:], back[:length], lags], axis=0))[0]]


def window_of(mats):
    return math.isqrt(mats[0].shape[0] * mats[0].shape[1])


def part_of(ref, size, rows, cols):
    height = ref.shape[0] // (size // LANES)
    blocks = range(cols[0] // LANES, cols[1] // LANES)
    return jnp.concatenate([ref[b * height + rows[0] : b * height + rows[1], :] for b in blocks], axis=1)


def dot_there(mats, x, start):
    size = window_of(mats)
    cols = (start, start + x.shape[0])
    return jnp.dot(part_of(mats[0], size, (0, size), cols), x, preferred_element_type=F32)


def dot_back(mats, rows, re, im):
    y = jnp.concatenate([re, im], axis=0).astype(BF16)
    size = y.shape[0]
    return jnp.dot(part_of(mats[1], size, rows, (0, size)), y, preferred_element_type=F32)


def column_blocks(group):
    width = min(256, group)
    return [slice(a, a + width) for a in range(0, group, width)]


def transform_taps(filter_taps, there):
    taps, group = filter_taps.shape
    size = window_of(there)

    def kernel(high_ref, low_ref, taps_ref, out_ref):
        cols = ((0, size), (0, taps))
        high, low = part_of(high_ref, size, *cols), part_of(low_ref, size, *cols)
        f = taps_ref[...]
        f_high = f.astype(BF16)
        f_low = (f - f_high.astype(F32)).astype(BF16)
        out = jnp.dot(high, f_low, preferred_element_type=F32) + jnp.dot(low, f_high, preferred_element_type=F32)
        out_ref[...] = out + jnp.dot(high, f_high, preferred_element_type=F32)

    return pl.pallas_call(
        kernel,
        in_specs=[VMEM] * 3,
        out_specs=VMEM,
        out_shape=jax.ShapeDtypeStruct((size, group), F32),
        compiler_params=pltpu.CompilerParams(vmem_limit_bytes=MID_VMEM),
        cost_estimate=pl.CostEstimate(flops=6 * size * taps * group, bytes_accessed=4 * size * group, transcendentals=0),
        name="taps",
    )(*there, filter_taps)


def in_row_order(out_ref, scratch, own, tp, paired):
    for b, index in enumerate(row_order(tp, paired)):
        out_ref[b * own : (b + 1) * own, :] = scratch[block_rows(index, own), :]


def filter_forward(spectra, before, query, conv_in_grad, out_grad, mats, weight, chunk, tp, paired):
    length, group = query.shape
    taps = before.shape[0]
    half = (length + taps) // 2
    start, depth = chunk[0], chunk[1] - chunk[0]
    step = step_rows(depth, 1)

    def kernel(there, back, p_ref, h_ref, before_ref, q_ref, cig_ref, grad_ref, w_ref, mixed_ref, qg_ref, fg_ref, c_ref,
               total_ref, sq, w_buf, w_sem):
        def compute(k, slot):
            at = pl.ds(pl.multiple_of(k * step, step), step)
            total_ref[:, at] = contract(qg_ref[...], w_buf[slot, 0])

        run = stream_weights([w_ref], w_buf, w_sem, start, depth // step, compute)
        mat_refs = (there, back)
        for cols in column_blocks(group):
            p = p_ref[:, cols] + dot_there(mat_refs, before_ref[:, cols], 0)
            c = dot_there(mat_refs, cig_ref[:, cols], 0)
            c_ref[:, cols] = c
            h = h_ref[:, cols]
            pr, pi, cr, ci, hr, hi = p[:half], p[half:], c[:half], c[half:], h[:half], h[half:]
            conv = dot_back(mat_refs, (0, length), pr * hr - pi * hi, pr * hi + pi * hr)
            mixed_ref[:, cols] = (q_ref[:, cols].astype(F32) * conv).astype(BF16)
            sq[:, cols] = (grad_ref[:, cols].astype(F32) * conv).astype(BF16)
            lags = (2 * length, 2 * length + taps)
            fg_ref[:, cols] = dot_back(mat_refs, lags, cr * pr + ci * pi, cr * pi - ci * pr).astype(BF16)
        in_row_order(qg_ref, sq, length // tp, tp, paired)
        run()

    full = jax.ShapeDtypeStruct((length, group), BF16)
    out_shape = [
        full,
        full,
        jax.ShapeDtypeStruct((taps, group), BF16),
        jax.ShapeDtypeStruct((length + taps, group), F32),
        jax.ShapeDtypeStruct((length, depth), F32),
    ]
    return pl.pallas_call(
        kernel,
        in_specs=[VMEM] * 8 + [ANYWHERE],
        out_specs=[VMEM] * 5,
        out_shape=out_shape,
        scratch_shapes=[pltpu.VMEM((length, group), BF16), *weight_scratch(1, step, group, 5)],
        compiler_params=pltpu.CompilerParams(vmem_limit_bytes=MIX_VMEM),
        cost_estimate=matmul_cost(length, depth + 2048, group, 1),
        name="conv",
    )(*mats, *spectra, before, query, conv_in_grad, out_grad, weight)


def filter_backward(spectra, after, keys, values, mats, weights, chunk, partial, tp, paired):
    length, group = keys.shape
    taps = after.shape[0]
    half = (length + taps) // 2
    start, depth = chunk[0], chunk[1] - chunk[0]
    step = step_rows(depth, 2)
    parts = 2 if paired else 1
    share = length // parts

    def kernel(*refs):
        there, back, c_ref, h_ref, after_ref, k_ref, v_ref, partial_ref, *refs = refs
        w_refs, out_refs, (kg_ref, vg_ref, sk, sv, w_buf, w_sem) = refs[:2], refs[2 : 2 + parts], refs[2 + parts :]

        def compute(k, slot):
            at = pl.ds(pl.multiple_of(k * step, step), step)
            total = partial_ref[:, at] + contract(kg_ref[...], w_buf[slot, 0]) + contract(vg_ref[...], w_buf[slot, 1])
            for i in range(parts):
                out_refs[i][:, at] = total[i * share : (i + 1) * share].astype(BF16)

        run = stream_weights(w_refs, w_buf, w_sem, start, depth // step, compute)
        mat_refs = (there, back)
        for cols in column_blocks(group):
            g = c_ref[:, cols] + dot_there(mat_refs, after_ref[:, cols], length)
            h = h_ref[:, cols]
            gr, gi, hr, hi = g[:half], g[half:], h[:half], h[half:]
            product_grad = dot_back(mat_refs, (length, 2 * length), hr * gr + hi * gi, hr * gi - hi * gr)
            sk[:, cols] = (product_grad * v_ref[:, cols].astype(F32)).astype(BF16)
            sv[:, cols] = (product_grad * k_ref[:, cols].astype(F32)).astype(BF16)
        in_row_order(kg_ref, sk, length // tp, tp, paired)
        in_row_order(vg_ref, sv, length // tp, tp, paired)
        run()

    full = jax.ShapeDtypeStruct((length, group), BF16)
    return pl.pallas_call(
        kernel,
        in_specs=[VMEM] * 8 + [ANYWHERE] * 2,
        out_specs=[VMEM] * (parts + 2),
        out_shape=[jax.ShapeDtypeStruct((share, depth), BF16)] * parts + [full] * 2,
        scratch_shapes=[pltpu.VMEM((length, group), BF16)] * 2 + weight_scratch(2, step, group, 5),
        compiler_params=pltpu.CompilerParams(vmem_limit_bytes=MIX_VMEM),
        cost_estimate=matmul_cost(length, depth + 1024, group, 2),
        name="conv_back",
    )(*mats, *spectra, after, keys, values, partial, *weights)


def project_back(grads, weights, chunk, parts, ready):
    rows, group = grads[0].shape
    count = len(grads)
    start, depth = chunk[0], chunk[1] - chunk[0]
    step = step_rows(depth, count)
    share = rows // parts
    n_in = 2 * count + len(ready)

    def kernel(*refs):
        g_refs, w_refs = refs[:count], refs[count : 2 * count]
        out_refs, (w_buf, w_sem) = refs[n_in : n_in + parts], refs[n_in + parts :]

        def compute(k, slot):
            at = pl.ds(pl.multiple_of(k * step, step), step)
            total = contract(g_refs[0][...], w_buf[slot, 0])
            for m in range(1, count):
                total = total + contract(g_refs[m][...], w_buf[slot, m])
            for i in range(parts):
                out_refs[i][:, at] = total[i * share : (i + 1) * share].astype(BF16)

        stream_weights(w_refs, w_buf, w_sem, start, depth // step, compute)()

    return pl.pallas_call(
        kernel,
        in_specs=[VMEM] * count + [ANYWHERE] * count + [VMEM] * len(ready),
        out_specs=[VMEM] * parts,
        out_shape=[jax.ShapeDtypeStruct((share, depth), BF16)] * parts,
        scratch_shapes=weight_scratch(count, step, group),
        compiler_params=pltpu.CompilerParams(vmem_limit_bytes=BWD_VMEM),
        cost_estimate=matmul_cost(rows, depth, group, count),
        name="project_back",
    )(*grads, *weights, *ready)


def on_device(inputs, query_weight, key_weight, value_weight, filter_taps, out_grad):
    tp = lax.axis_size("tp")
    paired = tp == 8
    own_rows, width = inputs.shape
    taps = filter_taps.shape[0]
    there, there_low, back = transforms(own_rows * tp, taps)
    mats = (there, back)
    h = transform_taps(filter_taps, (there, there_low))
    chunks = bounds(width, FWD_PARTS)
    gathered = gather_rows(inputs, chunks, paired, h)
    pair = (key_weight, value_weight)
    acc = None
    for i, (pieces, chunk) in enumerate(zip(gathered, chunks)):
        if paired:
            if i + 1 < len(chunks):
                pieces[0] = once(pieces[0], gathered[i + 1][0])
            pieces.append(swap(once(pieces[1], acc[0]) if acc else pieces[1], 0))
        if i + 1 < len(chunks):
            acc = project(pieces, (query_weight, *pair), chunk, acc, tp, paired, taps, False)
    keys, values, product, tail = project(pieces, pair, chunk, acc[1:], tp, paired, taps, True)
    before = from_behind(tail, "ctx", 1)
    query, conv_in_grad, head, p = project(
        pieces, (query_weight,), chunk, acc[:1], tp, paired, taps, True, out_grad, product, mats
    )
    after = from_behind(head, "ctx", -1)
    chunks = bounds(width, BWD_PARTS)
    mixed, query_grad, local_taps, c, partial = filter_forward(
        (p, h), before, query, conv_in_grad, out_grad, mats, query_weight, chunks[0], tp, paired
    )
    *piece, keys_grad, values_grad = filter_backward(
        (c, h), after, keys, values, mats, pair, chunks[0], partial, tp, paired
    )
    size = lax.axis_size("ctx")
    distances = [2**i for i in reversed(range(size.bit_length() - 1))] if size & (size - 1) == 0 else []
    pieces, totals = [piece], []
    grads, weights = (query_grad, keys_grad, values_grad), (query_weight, *pair)
    for i, chunk in enumerate(chunks[1:]):
        ready = []
        if paired:
            totals.append(chip_sums(pieces[i], own_rows))
            ready.append(totals[-1][1])
        pieces.append(project_back(grads, weights, chunk, 2 if paired else 1, ready))
    if distances:
        local_taps = add_pair(local_taps, "ctx", distances.pop(0), pieces[-1][0])
    if paired:
        summed, last = scatter_rows(pieces, totals, own_rows)
    else:
        summed = [lax.psum_scatter(p, "tp", scatter_dimension=0, tiled=True) for (p,) in pieces]
        last = summed
    for distance in distances:
        local_taps = add_pair(local_taps, "ctx", distance, *last)
    if size & (size - 1):
        local_taps = lax.psum(local_taps, "ctx")
    return mixed, jnp.concatenate(summed, axis=1), local_taps.astype(F32)


def solution(mesh):
    in_specs = (
        P(("ctx", "tp"), None),
        P(None, "tp"),
        P(None, "tp"),
        P(None, "tp"),
        P(None, "tp"),
        P("ctx", "tp"),
    )
    out_specs = (P("ctx", "tp"), P(("ctx", "tp"), None), P(None, "tp"))
    return jax.shard_map(
        on_device, mesh=mesh, in_specs=in_specs, out_specs=out_specs, check_vma=False
    )
```

```python
import math

import jax
import jax.numpy as jnp
import numpy as np
from jax import lax
from jax.experimental import pallas as pl
from jax.experimental.pallas import tpu as pltpu
from jax.sharding import PartitionSpec as P

F32 = jnp.float32
BF16 = jnp.bfloat16
FWD_VMEM = 42 * 2**20
BWD_VMEM = 42 * 2**20
MIX_VMEM = 35 * 2**20
MID_VMEM = 24 * 2**20
FWD_PARTS = (2, 6)
BWD_PARTS = (5, 3)


def bounds(width, parts):
    edges = np.cumsum((0,) + parts) * width // sum(parts)
    return [(int(a), int(b)) for a, b in zip(edges[:-1], edges[1:])]


def from_behind(block, axis, distance):
    devices = range(lax.axis_size(axis))
    route = [(i - distance, i) for i in devices if i - distance in devices]
    return lax.ppermute(block, axis, route)


def swap(block, way):
    offsets = {0: (1, 1), 1: (2, 4), 2: (4, 2)}[way]
    return lax.ppermute(block, "tp", [(i, i ^ offsets[i % 2]) for i in range(8)])


def row_order(tp, paired):
    if not paired:
        return list(range(tp))
    me = lax.axis_index("tp")
    first = 2 + 2 * (me % 2)
    second = 6 - first
    own = [me, me ^ first, me ^ second, me ^ 6]
    other = me ^ 1
    return own + [other, other ^ second, other ^ first, other ^ 6]


def block_rows(index, own):
    start = index * own
    return pl.ds(start if isinstance(start, int) else pl.multiple_of(start, own), own)


def once(value, *others):
    return lax.optimization_barrier((value, others))[0]


def add_up(*terms):
    return sum(t.astype(F32) for t in terms).astype(BF16)


def add_pair(total, axis, distance, *others):
    route = [(i, i ^ distance) for i in range(lax.axis_size(axis))]
    mine = total.astype(BF16)
    theirs = lax.ppermute(mine, axis, route)
    return mine.astype(F32) + (once(theirs, *others) if others else theirs).astype(F32)


def gather_rows(block, chunks, paired, *others):
    if not paired:
        return [[lax.all_gather(block[:, a:b], "tp", axis=0, tiled=True)] for a, b in chunks]
    first, pieces = once(swap(block, 1), *others), []
    for a, b in chunks:
        near = jnp.concatenate([block[:, a:b], first[:, a:b]], axis=0)
        pieces.append([near, swap(near, 2), swap(near, 0)])
    return pieces


def scatter_rows(pieces, totals, own):
    far, first = [swap(t[1], 2) for t in totals], []
    first.append(add_up(totals[0][0][own:], far[0][own:]))
    for piece in pieces[1:]:
        totals.append(chip_sums(piece, own, first[-1:]))
        far.append(swap(totals[-1][1], 2))
        first.append(add_up(totals[-1][0][own:], far[-1][own:]))
    near = [swap(f, 1) for f in first]
    return [add_up(t[:own], f[:own], n) for (t, _), f, n in zip(totals, far, near)], first


def chip_sums(piece, own, others=()):
    keep, give = piece
    theirs = swap(give, 0)
    if others:
        theirs = once(theirs, *others)
    far = add_up(keep[2 * own :], theirs[2 * own :])
    return add_up(keep[: 2 * own], theirs[: 2 * own]), far


def step_rows(depth, count):
    step = 512 if count > 1 else 1024
    while depth % step:
        step //= 2
    return step


def stream_weights(w_refs, w_buf, w_sem, start, steps, compute):
    count = len(w_refs)
    slots, _, step, _ = w_buf.shape
    ahead = min(slots - 1, steps)

    def copy(k, m):
        slot = lax.rem(k, slots)
        rows = pl.ds(start + k * step, step)
        return pltpu.make_async_copy(w_refs[m].at[rows, :], w_buf.at[slot, m], w_sem.at[slot, m])

    for k in range(ahead):
        for m in range(count):
            copy(k, m).start()

    def body(k, carry):
        @pl.when(k + ahead < steps)
        def _():
            for m in range(count):
                copy(k + ahead, m).start()

        for m in range(count):
            copy(k, m).wait()
        compute(k, lax.rem(k, slots))
        return carry

    return lambda: lax.fori_loop(0, steps, body, 0)


def weight_scratch(count, step, group, slots=3):
    return [pltpu.VMEM((slots, count, step, group), BF16), pltpu.SemaphoreType.DMA((slots, count))]


def contract(left, right):
    return lax.dot_general(left, right, (((1,), (1,)), ((), ())), preferred_element_type=F32)


def matmul_cost(rows, depth, group, count):
    return pl.CostEstimate(
        flops=2 * count * rows * depth * group, bytes_accessed=2 * count * depth * group, transcendentals=0
    )


VMEM = pl.BlockSpec(memory_space=pltpu.VMEM)
ANYWHERE = pl.BlockSpec(memory_space=pl.ANY)


def project(pieces, weights, chunk, acc, tp, paired, taps, finish, out_grad=None, product=None, mats=()):
    rows = sum(p.shape[0] for p in pieces)
    count = len(weights)
    group = weights[0].shape[1]
    start, depth = chunk[0], chunk[1] - chunk[0]
    step = step_rows(depth, count)
    own = rows // tp
    n_x = len(pieces)
    has_acc = acc is not None
    pair = count == 2

    def kernel(*refs):
        x_refs, w_refs, refs = refs[:n_x], refs[n_x : n_x + count], refs[n_x + count :]
        if has_acc:
            acc_refs, refs = refs[:count], refs[count:]
        if finish:
            if not pair:
                grad_ref, prod_ref, mat_refs, refs = refs[0], refs[1], refs[2 : 2 + len(mats)], refs[2 + len(mats) :]
            outs, made_ref, edge_ref, refs = refs[:count], refs[count], refs[count + 1], refs[count + 2 :]
            if not pair:
                spectrum_ref, refs = refs[0], refs[1:]
            totals = refs[:count]
        else:
            totals = refs[:count]
        x_buf, w_buf, w_sem = refs[-3:]

        def compute(k, slot):
            x = x_buf[:, pl.ds(pl.multiple_of(k * step, step), step)]
            for m in range(count):
                totals[m][...] += jnp.dot(x, w_buf[slot, m], preferred_element_type=F32)

        run = stream_weights(w_refs, w_buf, w_sem, start, depth // step, compute)
        at = 0
        for piece in x_refs:
            x_buf[at : at + piece.shape[0], :] = piece[...]
            at += piece.shape[0]
        for m in range(count):
            totals[m][...] = acc_refs[m][...] if has_acc else jnp.zeros_like(totals[m])
        if finish and not pair:
            for cols in column_blocks(group):
                spectrum_ref[:, cols] = dot_there(mat_refs, prod_ref[:, cols], taps)
        run()
        if finish:
            for b, index in enumerate(row_order(tp, paired)):
                here = block_rows(index, own)
                part = [total[b * own : (b + 1) * own, :].astype(BF16) for total in totals]
                for out, value in zip(outs, part):
                    out[here, :] = value
                other = part[1] if pair else grad_ref[here, :]
                made_ref[here, :] = (part[0].astype(F32) * other.astype(F32)).astype(BF16)
            edge_ref[...] = made_ref[rows - taps :, :] if pair else made_ref[:taps, :]

    in_specs = [VMEM] * n_x + [ANYWHERE] * count
    args = [*pieces, *weights]
    if has_acc:
        in_specs += [VMEM] * count
        args += acc
    totals = (rows, group)
    scratch = [pltpu.VMEM((rows, depth), BF16), *weight_scratch(count, step, group)]
    full = jax.ShapeDtypeStruct((rows, group), BF16)
    if finish:
        if not pair:
            in_specs += [VMEM] * (2 + len(mats))
            args += [out_grad, product, *mats]
        out_shape = [full] * (count + 1) + [jax.ShapeDtypeStruct((taps, group), BF16)]
        if not pair:
            out_shape.append(jax.ShapeDtypeStruct((rows + taps, group), F32))
        scratch = [pltpu.VMEM(totals, F32)] * count + scratch
    else:
        out_shape = [jax.ShapeDtypeStruct(totals, F32)] * count
    return pl.pallas_call(
        kernel,
        in_specs=in_specs,
        out_specs=[VMEM] * len(out_shape),
        out_shape=out_shape,
        scratch_shapes=scratch,
        compiler_params=pltpu.CompilerParams(vmem_limit_bytes=FWD_VMEM),
        cost_estimate=matmul_cost(rows, depth, group, count),
        name="project",
    )(*args)


LANES = 128


def constant(matrix):
    stacked = np.concatenate(np.split(matrix, matrix.shape[1] // LANES, axis=1), axis=0)
    high = stacked.astype(jnp.bfloat16)
    low = (stacked - high.astype(np.float64)).astype(jnp.bfloat16)
    return jnp.asarray(high), jnp.asarray(low)


def transforms(length, taps):
    size = length + taps
    angle = 2 * np.pi / size * np.outer(np.arange(size // 2) + 0.5, np.arange(size))
    there = np.concatenate([np.cos(angle), -np.sin(angle)], axis=0)
    back = there.T * (2.0 / size)
    lags = back[np.arange(taps, 0, -1)]
    return [*constant(there), constant(np.concatenate([back[taps:], back[:length], lags], axis=0))[0]]


def window_of(mats):
    return math.isqrt(mats[0].shape[0] * mats[0].shape[1])


def part_of(ref, size, rows, cols):
    height = ref.shape[0] // (size // LANES)
    blocks = range(cols[0] // LANES, cols[1] // LANES)
    return jnp.concatenate([ref[b * height + rows[0] : b * height + rows[1], :] for b in blocks], axis=1)


def dot_there(mats, x, start):
    size = window_of(mats)
    cols = (start, start + x.shape[0])
    return jnp.dot(part_of(mats[0], size, (0, size), cols), x, preferred_element_type=F32)


def dot_back(mats, rows, re, im):
    y = jnp.concatenate([re, im], axis=0).astype(BF16)
    size = y.shape[0]
    return jnp.dot(part_of(mats[1], size, rows, (0, size)), y, preferred_element_type=F32)


def column_blocks(group):
    width = min(256, group)
    return [slice(a, a + width) for a in range(0, group, width)]


def transform_taps(filter_taps, there):
    taps, group = filter_taps.shape
    size = window_of(there)

    def kernel(high_ref, low_ref, taps_ref, out_ref):
        cols = ((0, size), (0, taps))
        high, low = part_of(high_ref, size, *cols), part_of(low_ref, size, *cols)
        f = taps_ref[...]
        f_high = f.astype(BF16)
        f_low = (f - f_high.astype(F32)).astype(BF16)
        out = jnp.dot(high, f_low, preferred_element_type=F32) + jnp.dot(low, f_high, preferred_element_type=F32)
        out_ref[...] = out + jnp.dot(high, f_high, preferred_element_type=F32)

    return pl.pallas_call(
        kernel,
        in_specs=[VMEM] * 3,
        out_specs=VMEM,
        out_shape=jax.ShapeDtypeStruct((size, group), F32),
        compiler_params=pltpu.CompilerParams(vmem_limit_bytes=MID_VMEM),
        cost_estimate=pl.CostEstimate(flops=6 * size * taps * group, bytes_accessed=4 * size * group, transcendentals=0),
        name="taps",
    )(*there, filter_taps)


def in_row_order(out_ref, scratch, own, tp, paired):
    for b, index in enumerate(row_order(tp, paired)):
        out_ref[b * own : (b + 1) * own, :] = scratch[block_rows(index, own), :]


def filter_forward(spectra, before, query, conv_in_grad, out_grad, mats, weight, chunk, tp, paired):
    length, group = query.shape
    taps = before.shape[0]
    half = (length + taps) // 2
    start, depth = chunk[0], chunk[1] - chunk[0]
    step = step_rows(depth, 1)

    def kernel(there, back, p_ref, h_ref, before_ref, q_ref, cig_ref, grad_ref, w_ref, mixed_ref, qg_ref, fg_ref, c_ref,
               total_ref, sq, w_buf, w_sem):
        def compute(k, slot):
            at = pl.ds(pl.multiple_of(k * step, step), step)
            total_ref[:, at] = contract(qg_ref[...], w_buf[slot, 0])

        run = stream_weights([w_ref], w_buf, w_sem, start, depth // step, compute)
        mat_refs = (there, back)
        for cols in column_blocks(group):
            p = p_ref[:, cols] + dot_there(mat_refs, before_ref[:, cols], 0)
            c = dot_there(mat_refs, cig_ref[:, cols], 0)
            c_ref[:, cols] = c
            h = h_ref[:, cols]
            pr, pi, cr, ci, hr, hi = p[:half], p[half:], c[:half], c[half:], h[:half], h[half:]
            conv = dot_back(mat_refs, (0, length), pr * hr - pi * hi, pr * hi + pi * hr)
            mixed_ref[:, cols] = (q_ref[:, cols].astype(F32) * conv).astype(BF16)
            sq[:, cols] = (grad_ref[:, cols].astype(F32) * conv).astype(BF16)
            lags = (2 * length, 2 * length + taps)
            fg_ref[:, cols] = dot_back(mat_refs, lags, cr * pr + ci * pi, cr * pi - ci * pr).astype(BF16)
        in_row_order(qg_ref, sq, length // tp, tp, paired)
        run()

    full = jax.ShapeDtypeStruct((length, group), BF16)
    out_shape = [
        full,
        full,
        jax.ShapeDtypeStruct((taps, group), BF16),
        jax.ShapeDtypeStruct((length + taps, group), F32),
        jax.ShapeDtypeStruct((length, depth), F32),
    ]
    return pl.pallas_call(
        kernel,
        in_specs=[VMEM] * 8 + [ANYWHERE],
        out_specs=[VMEM] * 5,
        out_shape=out_shape,
        scratch_shapes=[pltpu.VMEM((length, group), BF16), *weight_scratch(1, step, group, 5)],
        compiler_params=pltpu.CompilerParams(vmem_limit_bytes=MIX_VMEM),
        cost_estimate=matmul_cost(length, depth + 2048, group, 1),
        name="conv",
    )(*mats, *spectra, before, query, conv_in_grad, out_grad, weight)


def filter_backward(spectra, after, keys, values, mats, weights, chunk, partial, tp, paired):
    length, group = keys.shape
    taps = after.shape[0]
    half = (length + taps) // 2
    start, depth = chunk[0], chunk[1] - chunk[0]
    step = step_rows(depth, 2)
    parts = 2 if paired else 1
    share = length // parts

    def kernel(*refs):
        there, back, c_ref, h_ref, after_ref, k_ref, v_ref, partial_ref, *refs = refs
        w_refs, out_refs, (kg_ref, vg_ref, sk, sv, w_buf, w_sem) = refs[:2], refs[2 : 2 + parts], refs[2 + parts :]

        def compute(k, slot):
            at = pl.ds(pl.multiple_of(k * step, step), step)
            seen = pl.ds(pl.multiple_of(start + k * step, step), step)
            total = partial_ref[:, seen] + contract(kg_ref[...], w_buf[slot, 0]) + contract(vg_ref[...], w_buf[slot, 1])
            for i in range(parts):
                out_refs[i][:, at] = total[i * share : (i + 1) * share].astype(BF16)

        run = stream_weights(w_refs, w_buf, w_sem, start, depth // step, compute)
        mat_refs = (there, back)
        for cols in column_blocks(group):
            g = c_ref[:, cols] + dot_there(mat_refs, after_ref[:, cols], length)
            h = h_ref[:, cols]
            gr, gi, hr, hi = g[:half], g[half:], h[:half], h[half:]
            product_grad = dot_back(mat_refs, (length, 2 * length), hr * gr + hi * gi, hr * gi - hi * gr)
            sk[:, cols] = (product_grad * v_ref[:, cols].astype(F32)).astype(BF16)
            sv[:, cols] = (product_grad * k_ref[:, cols].astype(F32)).astype(BF16)
        in_row_order(kg_ref, sk, length // tp, tp, paired)
        in_row_order(vg_ref, sv, length // tp, tp, paired)
        run()

    full = jax.ShapeDtypeStruct((length, group), BF16)
    return pl.pallas_call(
        kernel,
        in_specs=[VMEM] * 8 + [ANYWHERE] * 2,
        out_specs=[VMEM] * (parts + 2),
        out_shape=[jax.ShapeDtypeStruct((share, depth), BF16)] * parts + [full] * 2,
        scratch_shapes=[pltpu.VMEM((length, group), BF16)] * 2 + weight_scratch(2, step, group, 5),
        compiler_params=pltpu.CompilerParams(vmem_limit_bytes=MIX_VMEM),
        cost_estimate=matmul_cost(length, depth + 1024, group, 2),
        name="conv_back",
    )(*mats, *spectra, after, keys, values, partial, *weights)


def project_back(grads, weights, chunk, partial, parts, ready):
    rows, group = grads[0].shape
    count = len(grads)
    start, depth = chunk[0], chunk[1] - chunk[0]
    step = step_rows(depth, count)
    share = rows // parts
    n_in = 2 * count + 1 + len(ready)

    def kernel(*refs):
        g_refs, w_refs, partial_ref = refs[:count], refs[count : 2 * count], refs[2 * count]
        out_refs, (w_buf, w_sem) = refs[n_in : n_in + parts], refs[n_in + parts :]

        def compute(k, slot):
            at = pl.ds(pl.multiple_of(k * step, step), step)
            total = partial_ref[:, pl.ds(pl.multiple_of(start + k * step, step), step)]
            for m in range(count):
                total = total + contract(g_refs[m][...], w_buf[slot, m])
            for i in range(parts):
                out_refs[i][:, at] = total[i * share : (i + 1) * share].astype(BF16)

        stream_weights(w_refs, w_buf, w_sem, start, depth // step, compute)()

    return pl.pallas_call(
        kernel,
        in_specs=[VMEM] * count + [ANYWHERE] * count + [VMEM] * (1 + len(ready)),
        out_specs=[VMEM] * parts,
        out_shape=[jax.ShapeDtypeStruct((share, depth), BF16)] * parts,
        scratch_shapes=weight_scratch(count, step, group),
        compiler_params=pltpu.CompilerParams(vmem_limit_bytes=BWD_VMEM),
        cost_estimate=matmul_cost(rows, depth, group, count),
        name="project_back",
    )(*grads, *weights, partial, *ready)


def on_device(inputs, query_weight, key_weight, value_weight, filter_taps, out_grad):
    tp = lax.axis_size("tp")
    paired = tp == 8
    own_rows, width = inputs.shape
    taps = filter_taps.shape[0]
    there, there_low, back = transforms(own_rows * tp, taps)
    mats = (there, back)
    h = transform_taps(filter_taps, (there, there_low))
    chunks = bounds(width, FWD_PARTS)
    gathered = gather_rows(inputs, chunks, paired, h)
    pair = (key_weight, value_weight)
    acc = None
    for i, (pieces, chunk) in enumerate(zip(gathered, chunks)):
        if paired:
            if i + 1 < len(chunks):
                pieces[0] = once(pieces[0], gathered[i + 1][0])
            pieces.append(swap(once(pieces[1], acc[0]) if acc else pieces[1], 0))
        if i + 1 < len(chunks):
            acc = project(pieces, (query_weight, *pair), chunk, acc, tp, paired, taps, False)
    keys, values, product, tail = project(pieces, pair, chunk, acc[1:], tp, paired, taps, True)
    before = from_behind(tail, "ctx", 1)
    query, conv_in_grad, head, p = project(
        pieces, (query_weight,), chunk, acc[:1], tp, paired, taps, True, out_grad, product, mats
    )
    after = from_behind(head, "ctx", -1)
    chunks = bounds(width, BWD_PARTS)
    mixed, query_grad, local_taps, c, partial = filter_forward(
        (p, h), before, query, conv_in_grad, out_grad, mats, query_weight, (0, width), tp, paired
    )
    *piece, keys_grad, values_grad = filter_backward(
        (c, h), after, keys, values, mats, pair, chunks[0], partial, tp, paired
    )
    size = lax.axis_size("ctx")
    distances = [2**i for i in reversed(range(size.bit_length() - 1))] if size & (size - 1) == 0 else []
    pieces, totals = [piece], []
    grads = (keys_grad, values_grad)
    for i, chunk in enumerate(chunks[1:]):
        ready = []
        if paired:
            totals.append(chip_sums(pieces[i], own_rows))
            ready.append(totals[-1][1])
        pieces.append(project_back(grads, pair, chunk, partial, 2 if paired else 1, ready))
    if paired:
        summed, last = scatter_rows(pieces, totals, own_rows)
        if len(distances) > 1:
            local_taps = add_pair(local_taps, "ctx", distances.pop(0), totals[-1][1])
    else:
        summed = [lax.psum_scatter(p, "tp", scatter_dimension=0, tiled=True) for (p,) in pieces]
        last = summed
    for distance in distances:
        local_taps = add_pair(local_taps, "ctx", distance, *last)
    if size & (size - 1):
        local_taps = lax.psum(local_taps, "ctx")
    return mixed, jnp.concatenate(summed, axis=1), local_taps.astype(F32)


def solution(mesh):
    in_specs = (
        P(("ctx", "tp"), None),
        P(None, "tp"),
        P(None, "tp"),
        P(None, "tp"),
        P(None, "tp"),
        P("ctx", "tp"),
    )
    out_specs = (P("ctx", "tp"), P(("ctx", "tp"), None), P(None, "tp"))
    return jax.shard_map(
        on_device, mesh=mesh, in_specs=in_specs, out_specs=out_specs, check_vma=False
    )
```

```python
import math

import jax
import jax.numpy as jnp
import numpy as np
from jax import lax
from jax.experimental import pallas as pl
from jax.experimental.pallas import tpu as pltpu
from jax.sharding import PartitionSpec as P

F32 = jnp.float32
BF16 = jnp.bfloat16
FWD_VMEM = 42 * 2**20
BWD_VMEM = 42 * 2**20
MIX_VMEM = 35 * 2**20
MID_VMEM = 24 * 2**20
FWD_PARTS = (2, 6)
BWD_PARTS = (5, 3)


def bounds(width, parts):
    edges = np.cumsum((0,) + parts) * width // sum(parts)
    return [(int(a), int(b)) for a, b in zip(edges[:-1], edges[1:])]


def from_behind(block, axis, distance):
    devices = range(lax.axis_size(axis))
    route = [(i - distance, i) for i in devices if i - distance in devices]
    return lax.ppermute(block, axis, route)


def swap(block, way):
    offsets = {0: (1, 1), 1: (2, 4), 2: (4, 2)}[way]
    return lax.ppermute(block, "tp", [(i, i ^ offsets[i % 2]) for i in range(8)])


def row_order(tp, paired):
    if not paired:
        return list(range(tp))
    me = lax.axis_index("tp")
    first = 2 + 2 * (me % 2)
    second = 6 - first
    own = [me, me ^ first, me ^ second, me ^ 6]
    other = me ^ 1
    return own + [other, other ^ second, other ^ first, other ^ 6]


def block_rows(index, own):
    start = index * own
    return pl.ds(start if isinstance(start, int) else pl.multiple_of(start, own), own)


def once(value, *others):
    return lax.optimization_barrier((value, others))[0]


def add_up(*terms):
    return sum(t.astype(F32) for t in terms).astype(BF16)


def add_pair(total, axis, distance, *others):
    route = [(i, i ^ distance) for i in range(lax.axis_size(axis))]
    mine = total.astype(BF16)
    theirs = lax.ppermute(mine, axis, route)
    return mine.astype(F32) + (once(theirs, *others) if others else theirs).astype(F32)


def gather_rows(block, chunks, paired, *others):
    if not paired:
        return [[lax.all_gather(block[:, a:b], "tp", axis=0, tiled=True)] for a, b in chunks]
    first, pieces = once(swap(block, 1), *others), []
    for a, b in chunks:
        near = jnp.concatenate([block[:, a:b], first[:, a:b]], axis=0)
        pieces.append([near, swap(near, 2), swap(near, 0)])
    return pieces


def scatter_rows(pieces, totals, own):
    far, first = [swap(t[1], 2) for t in totals], []
    for piece in pieces[len(totals) :]:
        totals.append(chip_sums(piece, own))
        far.append(swap(totals[-1][1], 2))
    for i, (total, there) in enumerate(zip(totals, far)):
        there = once(there, totals[-1][1]) if i + 1 < len(totals) else there
        first.append(add_up(total[0][own:], there[own:]))
    near = [swap(f, 1) for f in first]
    return [add_up(t[:own], f[:own], n) for (t, _), f, n in zip(totals, far, near)], first


def chip_sums(piece, own, others=()):
    keep, give = piece
    theirs = swap(give, 0)
    if others:
        theirs = once(theirs, *others)
    far = add_up(keep[2 * own :], theirs[2 * own :])
    return add_up(keep[: 2 * own], theirs[: 2 * own]), far


def step_rows(depth, count):
    step = 512 if count > 1 else 1024
    while depth % step:
        step //= 2
    return step


def stream_weights(w_refs, w_buf, w_sem, start, steps, compute):
    count = len(w_refs)
    slots, _, step, _ = w_buf.shape
    ahead = min(slots - 1, steps)

    def copy(k, m):
        slot = lax.rem(k, slots)
        rows = pl.ds(start + k * step, step)
        return pltpu.make_async_copy(w_refs[m].at[rows, :], w_buf.at[slot, m], w_sem.at[slot, m])

    for k in range(ahead):
        for m in range(count):
            copy(k, m).start()

    def body(k, carry):
        @pl.when(k + ahead < steps)
        def _():
            for m in range(count):
                copy(k + ahead, m).start()

        for m in range(count):
            copy(k, m).wait()
        compute(k, lax.rem(k, slots))
        return carry

    return lambda: lax.fori_loop(0, steps, body, 0)


def weight_scratch(count, step, group, slots=3):
    return [pltpu.VMEM((slots, count, step, group), BF16), pltpu.SemaphoreType.DMA((slots, count))]


def contract(left, right):
    return lax.dot_general(left, right, (((1,), (1,)), ((), ())), preferred_element_type=F32)


def matmul_cost(rows, depth, group, count):
    return pl.CostEstimate(
        flops=2 * count * rows * depth * group, bytes_accessed=2 * count * depth * group, transcendentals=0
    )


VMEM = pl.BlockSpec(memory_space=pltpu.VMEM)
ANYWHERE = pl.BlockSpec(memory_space=pl.ANY)


def project(pieces, weights, chunk, acc, tp, paired, taps, finish, out_grad=None, product=None, mats=()):
    rows = sum(p.shape[0] for p in pieces)
    count = len(weights)
    group = weights[0].shape[1]
    start, depth = chunk[0], chunk[1] - chunk[0]
    step = step_rows(depth, count)
    own = rows // tp
    n_x = len(pieces)
    has_acc = acc is not None
    pair = count == 2

    def kernel(*refs):
        x_refs, w_refs, refs = refs[:n_x], refs[n_x : n_x + count], refs[n_x + count :]
        if has_acc:
            acc_refs, refs = refs[:count], refs[count:]
        if finish:
            if not pair:
                grad_ref, prod_ref, mat_refs, refs = refs[0], refs[1], refs[2 : 2 + len(mats)], refs[2 + len(mats) :]
            outs, made_ref, edge_ref, refs = refs[:count], refs[count], refs[count + 1], refs[count + 2 :]
            if not pair:
                spectrum_ref, refs = refs[0], refs[1:]
            totals = refs[:count]
        else:
            totals = refs[:count]
        x_buf, w_buf, w_sem = refs[-3:]

        def compute(k, slot):
            x = x_buf[:, pl.ds(pl.multiple_of(k * step, step), step)]
            for m in range(count):
                totals[m][...] += jnp.dot(x, w_buf[slot, m], preferred_element_type=F32)

        run = stream_weights(w_refs, w_buf, w_sem, start, depth // step, compute)
        at = 0
        for piece in x_refs:
            x_buf[at : at + piece.shape[0], :] = piece[...]
            at += piece.shape[0]
        for m in range(count):
            totals[m][...] = acc_refs[m][...] if has_acc else jnp.zeros_like(totals[m])
        if finish and not pair:
            for cols in column_blocks(group):
                spectrum_ref[:, cols] = dot_there(mat_refs, prod_ref[:, cols], taps)
        run()
        if finish:
            for b, index in enumerate(row_order(tp, paired)):
                here = block_rows(index, own)
                part = [total[b * own : (b + 1) * own, :].astype(BF16) for total in totals]
                for out, value in zip(outs, part):
                    out[here, :] = value
                other = part[1] if pair else grad_ref[here, :]
                made_ref[here, :] = (part[0].astype(F32) * other.astype(F32)).astype(BF16)
            edge_ref[...] = made_ref[rows - taps :, :] if pair else made_ref[:taps, :]

    in_specs = [VMEM] * n_x + [ANYWHERE] * count
    args = [*pieces, *weights]
    if has_acc:
        in_specs += [VMEM] * count
        args += acc
    totals = (rows, group)
    scratch = [pltpu.VMEM((rows, depth), BF16), *weight_scratch(count, step, group)]
    full = jax.ShapeDtypeStruct((rows, group), BF16)
    if finish:
        if not pair:
            in_specs += [VMEM] * (2 + len(mats))
            args += [out_grad, product, *mats]
        out_shape = [full] * (count + 1) + [jax.ShapeDtypeStruct((taps, group), BF16)]
        if not pair:
            out_shape.append(jax.ShapeDtypeStruct((rows + taps, group), F32))
        scratch = [pltpu.VMEM(totals, F32)] * count + scratch
    else:
        out_shape = [jax.ShapeDtypeStruct(totals, F32)] * count
    return pl.pallas_call(
        kernel,
        in_specs=in_specs,
        out_specs=[VMEM] * len(out_shape),
        out_shape=out_shape,
        scratch_shapes=scratch,
        compiler_params=pltpu.CompilerParams(vmem_limit_bytes=FWD_VMEM),
        cost_estimate=matmul_cost(rows, depth, group, count),
        name="project",
    )(*args)


LANES = 128


def constant(matrix):
    stacked = np.concatenate(np.split(matrix, matrix.shape[1] // LANES, axis=1), axis=0)
    high = stacked.astype(jnp.bfloat16)
    low = (stacked - high.astype(np.float64)).astype(jnp.bfloat16)
    return jnp.asarray(high), jnp.asarray(low)


def transforms(length, taps):
    size = length + taps
    angle = 2 * np.pi / size * np.outer(np.arange(size // 2) + 0.5, np.arange(size))
    there = np.concatenate([np.cos(angle), -np.sin(angle)], axis=0)
    back = there.T * (2.0 / size)
    lags = back[np.arange(taps, 0, -1)]
    return [*constant(there), constant(np.concatenate([back[taps:], back[:length], lags], axis=0))[0]]


def window_of(mats):
    return math.isqrt(mats[0].shape[0] * mats[0].shape[1])


def part_of(ref, size, rows, cols):
    height = ref.shape[0] // (size // LANES)
    blocks = range(cols[0] // LANES, cols[1] // LANES)
    return jnp.concatenate([ref[b * height + rows[0] : b * height + rows[1], :] for b in blocks], axis=1)


def dot_there(mats, x, start):
    size = window_of(mats)
    cols = (start, start + x.shape[0])
    return jnp.dot(part_of(mats[0], size, (0, size), cols), x, preferred_element_type=F32)


def dot_back(mats, rows, re, im):
    y = jnp.concatenate([re, im], axis=0).astype(BF16)
    size = y.shape[0]
    return jnp.dot(part_of(mats[1], size, rows, (0, size)), y, preferred_element_type=F32)


def column_blocks(group):
    width = min(256, group)
    return [slice(a, a + width) for a in range(0, group, width)]


def transform_taps(filter_taps, there):
    taps, group = filter_taps.shape
    size = window_of(there)

    def kernel(high_ref, low_ref, taps_ref, out_ref):
        cols = ((0, size), (0, taps))
        high, low = part_of(high_ref, size, *cols), part_of(low_ref, size, *cols)
        f = taps_ref[...]
        f_high = f.astype(BF16)
        f_low = (f - f_high.astype(F32)).astype(BF16)
        out = jnp.dot(high, f_low, preferred_element_type=F32) + jnp.dot(low, f_high, preferred_element_type=F32)
        out_ref[...] = out + jnp.dot(high, f_high, preferred_element_type=F32)

    return pl.pallas_call(
        kernel,
        in_specs=[VMEM] * 3,
        out_specs=VMEM,
        out_shape=jax.ShapeDtypeStruct((size, group), F32),
        compiler_params=pltpu.CompilerParams(vmem_limit_bytes=MID_VMEM),
        cost_estimate=pl.CostEstimate(flops=6 * size * taps * group, bytes_accessed=4 * size * group, transcendentals=0),
        name="taps",
    )(*there, filter_taps)


def in_row_order(out_ref, scratch, own, tp, paired):
    for b, index in enumerate(row_order(tp, paired)):
        out_ref[b * own : (b + 1) * own, :] = scratch[block_rows(index, own), :]


def filter_forward(spectra, before, query, conv_in_grad, out_grad, mats, weight, chunk, tp, paired):
    length, group = query.shape
    taps = before.shape[0]
    half = (length + taps) // 2
    start, depth = chunk[0], chunk[1] - chunk[0]
    step = step_rows(depth, 1)

    def kernel(there, back, p_ref, h_ref, before_ref, q_ref, cig_ref, grad_ref, w_ref, mixed_ref, qg_ref, fg_ref, c_ref,
               total_ref, sq, w_buf, w_sem):
        def compute(k, slot):
            at = pl.ds(pl.multiple_of(k * step, step), step)
            total_ref[:, at] = contract(qg_ref[...], w_buf[slot, 0])

        run = stream_weights([w_ref], w_buf, w_sem, start, depth // step, compute)
        mat_refs = (there, back)
        for cols in column_blocks(group):
            p = p_ref[:, cols] + dot_there(mat_refs, before_ref[:, cols], 0)
            c = dot_there(mat_refs, cig_ref[:, cols], 0)
            c_ref[:, cols] = c
            h = h_ref[:, cols]
            pr, pi, cr, ci, hr, hi = p[:half], p[half:], c[:half], c[half:], h[:half], h[half:]
            conv = dot_back(mat_refs, (0, length), pr * hr - pi * hi, pr * hi + pi * hr)
            mixed_ref[:, cols] = (q_ref[:, cols].astype(F32) * conv).astype(BF16)
            sq[:, cols] = (grad_ref[:, cols].astype(F32) * conv).astype(BF16)
            lags = (2 * length, 2 * length + taps)
            fg_ref[:, cols] = dot_back(mat_refs, lags, cr * pr + ci * pi, cr * pi - ci * pr).astype(BF16)
        in_row_order(qg_ref, sq, length // tp, tp, paired)
        run()

    full = jax.ShapeDtypeStruct((length, group), BF16)
    out_shape = [
        full,
        full,
        jax.ShapeDtypeStruct((taps, group), BF16),
        jax.ShapeDtypeStruct((length + taps, group), F32),
        jax.ShapeDtypeStruct((length, depth), F32),
    ]
    return pl.pallas_call(
        kernel,
        in_specs=[VMEM] * 8 + [ANYWHERE],
        out_specs=[VMEM] * 5,
        out_shape=out_shape,
        scratch_shapes=[pltpu.VMEM((length, group), BF16), *weight_scratch(1, step, group, 5)],
        compiler_params=pltpu.CompilerParams(vmem_limit_bytes=MIX_VMEM),
        cost_estimate=matmul_cost(length, depth + 2048, group, 1),
        name="conv",
    )(*mats, *spectra, before, query, conv_in_grad, out_grad, weight)


def filter_backward(spectra, after, keys, values, mats, weights, chunk, partial, tp, paired):
    length, group = keys.shape
    taps = after.shape[0]
    half = (length + taps) // 2
    start, depth = chunk[0], chunk[1] - chunk[0]
    step = step_rows(depth, 2)
    parts = 2 if paired else 1
    share = length // parts

    def kernel(*refs):
        there, back, c_ref, h_ref, after_ref, k_ref, v_ref, partial_ref, *refs = refs
        w_refs, out_refs, (kg_ref, vg_ref, sk, sv, w_buf, w_sem) = refs[:2], refs[2 : 2 + parts], refs[2 + parts :]

        def compute(k, slot):
            at = pl.ds(pl.multiple_of(k * step, step), step)
            seen = pl.ds(pl.multiple_of(start + k * step, step), step)
            total = partial_ref[:, seen] + contract(kg_ref[...], w_buf[slot, 0]) + contract(vg_ref[...], w_buf[slot, 1])
            for i in range(parts):
                out_refs[i][:, at] = total[i * share : (i + 1) * share].astype(BF16)

        run = stream_weights(w_refs, w_buf, w_sem, start, depth // step, compute)
        mat_refs = (there, back)
        for cols in column_blocks(group):
            g = c_ref[:, cols] + dot_there(mat_refs, after_ref[:, cols], length)
            h = h_ref[:, cols]
            gr, gi, hr, hi = g[:half], g[half:], h[:half], h[half:]
            product_grad = dot_back(mat_refs, (length, 2 * length), hr * gr + hi * gi, hr * gi - hi * gr)
            sk[:, cols] = (product_grad * v_ref[:, cols].astype(F32)).astype(BF16)
            sv[:, cols] = (product_grad * k_ref[:, cols].astype(F32)).astype(BF16)
        in_row_order(kg_ref, sk, length // tp, tp, paired)
        in_row_order(vg_ref, sv, length // tp, tp, paired)
        run()

    full = jax.ShapeDtypeStruct((length, group), BF16)
    return pl.pallas_call(
        kernel,
        in_specs=[VMEM] * 8 + [ANYWHERE] * 2,
        out_specs=[VMEM] * (parts + 2),
        out_shape=[jax.ShapeDtypeStruct((share, depth), BF16)] * parts + [full] * 2,
        scratch_shapes=[pltpu.VMEM((length, group), BF16)] * 2 + weight_scratch(2, step, group, 5),
        compiler_params=pltpu.CompilerParams(vmem_limit_bytes=MIX_VMEM),
        cost_estimate=matmul_cost(length, depth + 1024, group, 2),
        name="conv_back",
    )(*mats, *spectra, after, keys, values, partial, *weights)


def project_back(grads, weights, chunk, partial, parts, ready):
    rows, group = grads[0].shape
    count = len(grads)
    start, depth = chunk[0], chunk[1] - chunk[0]
    step = step_rows(depth, count)
    share = rows // parts
    n_in = 2 * count + 1 + len(ready)

    def kernel(*refs):
        g_refs, w_refs, partial_ref = refs[:count], refs[count : 2 * count], refs[2 * count]
        out_refs, (w_buf, w_sem) = refs[n_in : n_in + parts], refs[n_in + parts :]

        def compute(k, slot):
            at = pl.ds(pl.multiple_of(k * step, step), step)
            total = partial_ref[:, pl.ds(pl.multiple_of(start + k * step, step), step)]
            for m in range(count):
                total = total + contract(g_refs[m][...], w_buf[slot, m])
            for i in range(parts):
                out_refs[i][:, at] = total[i * share : (i + 1) * share].astype(BF16)

        stream_weights(w_refs, w_buf, w_sem, start, depth // step, compute)()

    return pl.pallas_call(
        kernel,
        in_specs=[VMEM] * count + [ANYWHERE] * count + [VMEM] * (1 + len(ready)),
        out_specs=[VMEM] * parts,
        out_shape=[jax.ShapeDtypeStruct((share, depth), BF16)] * parts,
        scratch_shapes=weight_scratch(count, step, group),
        compiler_params=pltpu.CompilerParams(vmem_limit_bytes=BWD_VMEM),
        cost_estimate=matmul_cost(rows, depth, group, count),
        name="project_back",
    )(*grads, *weights, partial, *ready)


def on_device(inputs, query_weight, key_weight, value_weight, filter_taps, out_grad):
    tp = lax.axis_size("tp")
    paired = tp == 8
    own_rows, width = inputs.shape
    taps = filter_taps.shape[0]
    there, there_low, back = transforms(own_rows * tp, taps)
    mats = (there, back)
    h = transform_taps(filter_taps, (there, there_low))
    chunks = bounds(width, FWD_PARTS)
    gathered = gather_rows(inputs, chunks, paired, h)
    pair = (key_weight, value_weight)
    acc = None
    for i, (pieces, chunk) in enumerate(zip(gathered, chunks)):
        if paired:
            if i + 1 < len(chunks):
                pieces[0] = once(pieces[0], gathered[i + 1][0])
            pieces.append(swap(once(pieces[1], acc[0]) if acc else pieces[1], 0))
        if i + 1 < len(chunks):
            acc = project(pieces, (query_weight, *pair), chunk, acc, tp, paired, taps, False)
    keys, values, product, tail = project(pieces, pair, chunk, acc[1:], tp, paired, taps, True)
    before = from_behind(tail, "ctx", 1)
    query, conv_in_grad, head, p = project(
        pieces, (query_weight,), chunk, acc[:1], tp, paired, taps, True, out_grad, product, mats
    )
    after = from_behind(head, "ctx", -1)
    chunks = bounds(width, BWD_PARTS)
    mixed, query_grad, local_taps, c, partial = filter_forward(
        (p, h), before, query, conv_in_grad, out_grad, mats, query_weight, (0, width), tp, paired
    )
    *piece, keys_grad, values_grad = filter_backward(
        (c, h), after, keys, values, mats, pair, chunks[0], partial, tp, paired
    )
    size = lax.axis_size("ctx")
    distances = [2**i for i in reversed(range(size.bit_length() - 1))] if size & (size - 1) == 0 else []
    pieces, totals = [piece], []
    grads = (keys_grad, values_grad)
    for i, chunk in enumerate(chunks[1:]):
        ready = []
        if paired:
            totals.append(chip_sums(pieces[i], own_rows))
            ready.append(totals[-1][1])
        pieces.append(project_back(grads, pair, chunk, partial, 2 if paired else 1, ready))
    if paired:
        summed, last = scatter_rows(pieces, totals, own_rows)
        if len(distances) > 1:
            local_taps = add_pair(local_taps, "ctx", distances.pop(0), totals[-1][1])
    else:
        summed = [lax.psum_scatter(p, "tp", scatter_dimension=0, tiled=True) for (p,) in pieces]
        last = summed
    for distance in distances:
        local_taps = add_pair(local_taps, "ctx", distance, *last)
    if size & (size - 1):
        local_taps = lax.psum(local_taps, "ctx")
    return mixed, jnp.concatenate(summed, axis=1), local_taps.astype(F32)


def solution(mesh):
    in_specs = (
        P(("ctx", "tp"), None),
        P(None, "tp"),
        P(None, "tp"),
        P(None, "tp"),
        P(None, "tp"),
        P("ctx", "tp"),
    )
    out_specs = (P("ctx", "tp"), P(("ctx", "tp"), None), P(None, "tp"))
    return jax.shard_map(
        on_device, mesh=mesh, in_specs=in_specs, out_specs=out_specs, check_vma=False
    )
```
